256 devices in a mesh: tm: 16 (over x, y_hi, core), space: 16 (over y_lo, z).
Axes of the slice: x: 4, y: 4 (y_hi: 2, y_lo: 2; y = y_hi * 2 + y_lo), z: 8, core: 2. Of those that a mesh axis runs over, the one named last changes fastest.
Arguments:
- start_guess: float32 [16, 16, 192, 384], P('tm', 'space'), may hold values from -6 to 6
- material: int32 [16, 192, 384], P('space'), may hold values from 0 to 2
- channel: int32 [16, 192, 384], P('space'), may hold values from 0 to 32, as said below
- coolant_temp: float32 [16, 32], P('tm'), may hold values from -2 to 1
- htc_index: int32 [16, 32], P('tm'), may hold values from 0 to 15
- htc_levels: float32 [16], replicated, may hold values from 0.2 to 8
- melt_steps: int32 [16], P('tm'), may hold values from 0 to 4
Outputs:
- new_start: float32 [16, 16, 192, 384], P('tm', 'space')
- fine_end: float32 [16, 16, 192, 384], P('tm', 'space')
The draws below stay inside these ranges and needn't reach their ends.
Inputs may be any that keep to these rules, and one draw needn't show every extreme that they name: 0 marks a cell without a cooling channel; 1 to 32 name the channel segment whose face the cell lies on.
All inputs are finite; a program needn't handle non-finite values.
Results may differ from the reference program's by a relative error of at most 0.0003.
Values sent between devices are 32-bit elements; how exact they have to be, the bound alone decides.
No kernel may reach another device: no remote copies, remote signals or barrier semaphores. Data moves between devices by JAX's collectives and lax.ppermute only.
A program may use at most 64 MiB of HBM per device.

```python
import math
import jax
import jax.numpy as jnp
from jax import lax

CY = 192
CZ = 384
STEPS = 4
SWEEPS = 6
SEGS = 32
LEVELS = 16
NT = 16
NX = 16
N_TM = 16


def draw_channel(key, part):
    key = jax.random.fold_in(key, 7)
    key_open, key_segment = jax.random.split(key)
    opened = jax.random.randint(key_open, (NX, CY, CZ), 0, 4)
    segment = jax.random.randint(key_segment, (NX, CY, CZ), 1, SEGS + 1)
    return jnp.where(opened == 0, segment, 0).astype(jnp.int32)


def place_ends(entries, stream_key, low, high):
    index_at = [jax.random.randint(jax.random.fold_in(stream_key, axis), (), 0, length) for axis, length in enumerate(entries.shape)]
    widest = entries.shape.index(max(entries.shape))
    next_to = index_at[:widest] + [(index_at[widest] + 1) % entries.shape[widest]] + index_at[widest + 1:]
    return entries.at[tuple(index_at)].set(low).at[tuple(next_to)].set(high)


def block_levels(key, dims, cuts, least, top_value):
    gain, own = 1.0, jax.random.fold_in(key, 6)
    for axis_at, parts in cuts:
        steps = jnp.exp(jax.random.uniform(jax.random.fold_in(own, axis_at), (parts,), jnp.float32, least / len(cuts), top_value / len(cuts)))
        gain = gain * jnp.repeat(steps, dims[axis_at] // parts).reshape([-1 if axis == axis_at else 1 for axis in range(len(dims))])
    return gain


def normal_values(stream_key, extent, spread, limit, shards=(), held_as=jnp.bfloat16):
    result = spread * jax.random.normal(stream_key, extent, jnp.float32)
    if shards:
        result = result * block_levels(stream_key, extent, shards, -0.22, 0.18)
    return jnp.clip(result, -limit, limit).astype(held_as)


def setup_inputs(seed: int = 0) -> dict:
    splits = jax.random.split(jax.random.key(seed), 8)
    start_guess = normal_values(splits[0], (NT, NX, CY, CZ), 1.0, 6.0, ((0, 16), (1, 16)), jnp.float32)
    material = place_ends(jax.random.randint(splits[1], (NX, CY, CZ), 0, 3), jax.random.fold_in(splits[1], 1), 0, 2).astype(jnp.int32)
    channel = draw_channel(jax.random.fold_in(splits[7], 71), 0)
    coolant_temp = jnp.clip(-2.0 + 3.0 * jax.random.uniform(splits[3], (NT, SEGS), jnp.float32) ** block_levels(splits[3], (NT, SEGS), ((0, 16),), -0.2, 0.2), -2.0, 1.0)
    htc_index = place_ends(jax.random.randint(splits[4], (NT, SEGS), 0, LEVELS), jax.random.fold_in(splits[4], 1), 0, LEVELS - 1).astype(jnp.int32)
    htc_levels = jnp.clip(jnp.exp(jax.random.uniform(splits[5], (LEVELS,), jnp.float32, math.log(0.2), math.log(8.0))), 0.2, 8.0)
    melt_steps = place_ends(jax.random.randint(splits[6], (NT,), 0, STEPS + 1), jax.random.fold_in(splits[6], 1), 0, STEPS).astype(jnp.int32)
    return dict(start_guess=start_guess, material=material, channel=channel, coolant_temp=coolant_temp, htc_index=htc_index, htc_levels=htc_levels, melt_steps=melt_steps)


time_step = 0.25
melt_rate = 4.0
lam_high = 1.0 + time_step * (12.0 * 3.0 + 8.0)
cheb_center = 0.5 * (lam_high + 1.0)
cheb_half = 0.5 * (lam_high - 1.0)
cheb_ratio = cheb_center / cheb_half


def conductivity(material):
    return jnp.where(material == 0, 1.0, jnp.where(material == 1, 3.0, 0.6)).astype(jnp.float32)


def face_terms(padded):
    inner = padded[1:-1, 1:-1, 1:-1]
    return ((inner + padded[2:, 1:-1, 1:-1]) * 0.5, (inner + padded[:-2, 1:-1, 1:-1]) * 0.5,
            (inner + padded[1:-1, 2:, 1:-1]) * 0.5, (inner + padded[1:-1, :-2, 1:-1]) * 0.5,
            (inner + padded[1:-1, 1:-1, 2:]) * 0.5, (inner + padded[1:-1, 1:-1, :-2]) * 0.5)


def coefficients(face_set, heat_rate):
    x_high, x_low, y_high, y_low, z_high, z_low = face_set
    diagonal = 1.0 + time_step * (x_high + x_low + y_high + y_low + z_high + z_low + heat_rate)
    return face_set, diagonal


def stencil(field_in, padded, coeffs):
    face_set, diagonal = coeffs
    x_high, x_low, y_high, y_low, z_high, z_low = face_set
    beside = x_high * padded[2:, 1:-1, 1:-1] + x_low * padded[:-2, 1:-1, 1:-1]
    beside = beside + y_high * padded[1:-1, 2:, 1:-1] + y_low * padded[1:-1, :-2, 1:-1]
    beside = beside + z_high * padded[1:-1, 1:-1, 2:] + z_low * padded[1:-1, 1:-1, :-2]
    return diagonal * field_in - time_step * beside


def implicit_step(previous, source, operator):
    rhs_field = previous + time_step * source
    iterate = previous
    remain = rhs_field - operator(iterate)
    update = remain / cheb_center
    cheb_rho = 1.0 / cheb_ratio
    iterate = iterate + update
    for sweep_index in range(SWEEPS - 1):
        remain = remain - operator(update)
        rho_next = 1.0 / (2.0 * cheb_ratio - cheb_rho)
        update = (rho_next * cheb_rho) * update + (2.0 * rho_next / cheb_half) * remain
        cheb_rho = rho_next
        iterate = iterate + update
    return iterate


def propagate(start_field, heat_in, cavity, melt_count, operator):
    state_now = start_field
    for step_index in range(STEPS):
        source = heat_in + jnp.where(step_index < melt_count, melt_rate, 0.0) * cavity
        state_now = implicit_step(state_now, source, operator)
    return state_now


def segment_tables(seg_temps, indices, htc_levels):
    level_ids = jnp.arange(htc_levels.shape[0], dtype=jnp.int32)
    picked = jnp.sum(jnp.where(indices[:, None] == level_ids[None, :], htc_levels[None, :], 0.0), axis=1)
    zero_row = jnp.zeros((1,), jnp.float32)
    return jnp.concatenate([zero_row, picked]), jnp.concatenate([zero_row, picked * seg_temps])


def reference(start_guess, material, channel, coolant_temp, htc_index, htc_levels, melt_steps):
    conduct = conductivity(material)
    face_set = face_terms(jnp.pad(conduct, 1, mode="edge"))
    cavity = (material == 2).astype(jnp.float32)
    lump_rate = 0.1 / N_TM
    coarse_span = STEPS * time_step

    def one_group(inputs):
        start_field, seg_temps, indices, melt_count = inputs
        rate_table, heat_table = segment_tables(seg_temps, indices, htc_levels)
        heat_rate = rate_table[channel]
        heat_in = heat_table[channel]
        coeffs = coefficients(face_set, heat_rate)

        def operator(field_in):
            return stencil(field_in, jnp.pad(field_in, 1), coeffs)

        fine_field = propagate(start_field, heat_in, cavity, melt_count, operator)
        multiplier = 1.0 / (1.0 + coarse_span * (heat_rate + lump_rate * conduct))
        return fine_field, multiplier

    fine_end, multiplier = lax.map(one_group, (start_guess, coolant_temp, htc_index, melt_steps))
    offset = fine_end - multiplier * start_guess

    def chain_step(chain_state, map_pair):
        gain_acc, shift_acc = chain_state
        return (map_pair[0] * gain_acc, map_pair[0] * shift_acc + map_pair[1]), chain_state

    unit_gain = jnp.ones(start_guess.shape[1:], jnp.float32)
    zero_shift = jnp.zeros(start_guess.shape[1:], jnp.float32)
    full_cycle, prefix = lax.scan(chain_step, (unit_gain, zero_shift), (multiplier, offset))
    anchor = full_cycle[1] / (1.0 - full_cycle[0])
    new_start = prefix[0] * anchor[None] + prefix[1]
    return new_start, fine_end
```

```python
import functools

import jax
import jax.numpy as jnp
from jax import lax
from jax.experimental import pallas as pl
from jax.experimental.pallas import tpu as pltpu
from jax.sharding import PartitionSpec as P

NT = 16
NX = 16
CY = 192
CZ = 384
STEPS = 4
SWEEPS = 6
SEGS = 32
LEVELS = 16

time_step = 0.25
melt_rate = 4.0
lam_high = 1.0 + time_step * (12.0 * 3.0 + 8.0)
cheb_center = 0.5 * (lam_high + 1.0)
cheb_half = 0.5 * (lam_high - 1.0)
cheb_ratio = cheb_center / cheb_half
lump_rate = 0.1 / NT

ZB = 48
HALO = STEPS * SWEEPS
ZE = ZB + 2 * HALO
YB = 96
ROWS = 40
UNROLL = 4


def chebyshev():
    rho = 1.0 / cheb_ratio
    pairs = []
    for _ in range(SWEEPS - 1):
        rho_next = 1.0 / (2.0 * cheb_ratio - rho)
        pairs.append((rho_next * rho, 2.0 * rho_next / cheb_half))
        rho = rho_next
    return pairs


def lanes(rows):
    return lax.broadcasted_iota(jnp.int32, (rows, 128), 1)


def lookup(row, index):
    return jnp.take_along_axis(jnp.broadcast_to(row, index.shape), index, axis=1, mode="promise_in_bounds")


def conductivity(material):
    return jnp.where(material == 0.0, 1.0, jnp.where(material == 1.0, 3.0, 0.6)).astype(jnp.float32)


def window(plane, by):
    part = plane[64 * by : 64 * by + 128, :].T
    return part if by == 0 else pltpu.roll(part, 96, 1)


def fold(block):
    tail = block[40:48]
    side = [pltpu.roll(tail, 96, 1), pltpu.roll(tail, 64, 1), pltpu.roll(tail, 32, 1)]
    side = side + [jnp.zeros((8, 128), jnp.float32)] * 2
    lane = lanes(8)
    return [jnp.where(lane < YB, block[8 * i : 8 * i + 8], side[i]) for i in range(5)]


def unfold(folded):
    lane = lanes(8)
    tail = jnp.where(
        lane < 32,
        pltpu.roll(folded[0:8], 32, 1),
        jnp.where(lane < 64, pltpu.roll(folded[8:16], 64, 1), pltpu.roll(folded[16:24], 96, 1)),
    )
    return [folded[8 * i : 8 * i + 8] for i in range(5)] + [tail]


def pack_kernel(
    place, levels, start, material, channel, coolant, index, packed, scaled, cells, base, tables, row
):
    core = place[0]
    row[...] = jnp.zeros_like(row)
    row[0:1, 0:SEGS] = index[...]
    ids = row[0:1, :]
    picked = jnp.zeros((1, 128), jnp.float32)
    for level in range(LEVELS):
        picked = jnp.where(ids == level, levels[level], picked)
    lane_row = lanes(1)
    picked = jnp.where(lane_row < SEGS, picked, 0.0)
    tables[...] = jnp.zeros_like(tables)
    tables[1:2, 0:SEGS] = coolant[...]
    temps = tables[1:2, :]
    rate_table = pltpu.roll(picked, 1, 1)
    tables[0:1, :] = rate_table
    tables[1:2, :] = pltpu.roll(picked * temps, 1, 1)
    negated = -pltpu.roll(picked, YB, 1)
    lane = lanes(8)
    sub = lax.broadcasted_iota(jnp.int32, (8, 128), 0)
    for by in range(2):
        field = window(start[...], by)
        mat = window(material[...].astype(jnp.float32), by)
        seg = window(channel[...].astype(jnp.float32), by)
        label = jnp.where(core == 0, mat, seg)
        for bz in range(8):
            b = by * 8 + bz
            at = slice(ZB * bz, ZB * bz + ZB)
            packed[b, 0] = field[at]
            packed[b, 1] = label[at]
            f, m, s = fold(field[at]), fold(mat[at]), fold(seg[at])
            for i in range(5):
                ids = s[i].astype(jnp.int32)
                lump = 1.0 + lump_rate * conductivity(m[i])
                value = f[i] / (lump + lookup(rate_table, ids))
                if i == 3:
                    value = jnp.where((sub == 0) & (lane >= YB), negated, value)
                scaled[b, 8 * i : 8 * i + 8] = value
                cells[b, 8 * i : 8 * i + 8] = ids
                base[b, 8 * i : 8 * i + 8] = lump


def fine_kernel(
    place, received, up, down, up_mc, down_mc, other, other_up, other_down, tables, out,
    xa, xb, rhs, kz, ky, kx, diag, heat, cavity, cond,
):
    core, bz, by, melt = place[0], place[1], place[2], place[3]
    lane = lanes(8)
    sub = lax.broadcasted_iota(jnp.int32, (8, 128), 0)
    rate_table = tables[0:1, :]
    heat_table = tables[1:2, :]

    def load(z, field, mine, theirs):
        for half in range(2):
            to = slice(8 * half, 8 * half + 8)
            xa[z, to] = field(half)
            a, b = mine(half), theirs(half)
            mat = jnp.where(core == 0, a, b)
            seg = jnp.where(core == 0, b, a).astype(jnp.int32)
            cond[z, to] = conductivity(mat)
            cavity[z, to] = jnp.where(mat == 2.0, time_step * melt_rate, 0.0)
            heat[z, to] = time_step * lookup(heat_table, seg)
            diag[z, to] = 1.0 + time_step * lookup(rate_table, seg)

    def strided(ref, pitch, at):
        return lambda half: ref[pl.ds(half * pitch + at, 8, stride=2 * pitch), :]

    def load_rim(z, carry):
        load(z, strided(up, HALO, z), strided(up_mc, HALO, z), strided(other_up, HALO, z))
        load(
            z + HALO + ZB,
            strided(down, HALO, z),
            strided(down_mc, HALO, z),
            strided(other_down, HALO, z),
        )
        return carry

    def load_core(z, carry):
        load(
            z + HALO,
            strided(received, 2 * ZB, z),
            strided(received, 2 * ZB, z + ZB),
            strided(other, ZB, z),
        )
        return carry

    lax.fori_loop(0, HALO, load_rim, 0, unroll=2)
    lax.fori_loop(0, ZB, load_core, 0, unroll=2)

    last = jnp.where(by == 0, 127, YB - 1)
    first = jnp.where(by == 0, 0, YB)
    y_inner = jnp.where(lane == last, 0.0, 1.0)
    y_edge = jnp.where((lane == last) | (lane == first), time_step, 0.0)
    x_inner = jnp.where(sub == 7, 0.0, 1.0)
    low_edge = jnp.where(sub == 0, time_step, 0.0)
    high_edge = jnp.where(sub == 7, time_step, 0.0)
    z0 = bz * ZB - HALO
    half_step = 0.5 * time_step

    def faces(z, carry):
        gz = z + z0
        inner = jnp.where((gz == -1) | (gz == CZ - 1), 0.0, half_step)
        z_edge = jnp.where((gz == 0) | (gz == CZ - 1), time_step, 0.0)
        even, odd = cond[z, 0:8], cond[z, 8:16]
        between = half_step * (even + odd)
        beyond = half_step * x_inner * (odd + pltpu.roll(even, 7, 0))
        kx[z, 0:8] = between
        kx[z, 8:16] = beyond
        across = (between + pltpu.roll(beyond, 1, 0), between + beyond)
        edges = (low_edge, high_edge)
        out_carry = []
        for half in range(2):
            at = slice(8 * half, 8 * half + 8)
            c = (even, odd)[half]
            high = inner * (c + cond[z + 1, at])
            kz[z, at] = high
            side = half_step * y_inner * (c + pltpu.roll(c, 127, 1))
            ky[z, at] = side
            total = across[half] + side + pltpu.roll(side, 1, 1) + high + carry[half]
            total = total + c * (edges[half] + y_edge + z_edge)
            diag[z, at] = diag[z, at] + total
            out_carry.append(high)
        return tuple(out_carry)

    zero = jnp.zeros((8, 128), jnp.float32)
    lax.fori_loop(0, ZE - 1, faces, (zero, zero), unroll=2)

    pairs = chebyshev()

    def apply(new, now, step, sweep):
        j = step * SWEEPS + sweep
        begin = j + 1
        trips = -(-(ZE - 2 - 2 * j) // UNROLL)
        heated = jnp.where(step < melt, 1.0, 0.0)

        def rows(i, carry):
            below, here, flow = carry
            base = begin + i * UNROLL
            for u in range(UNROLL):
                z = base + u
                above = (now[z + 1, 0:8], now[z + 1, 8:16])
                even, odd = here
                between, beyond = kx[z, 0:8], kx[z, 8:16]
                across = (
                    between * odd + pltpu.roll(beyond * odd, 1, 0),
                    between * even + beyond * pltpu.roll(even, 7, 0),
                )
                next_flow = []
                for half in range(2):
                    at = slice(8 * half, 8 * half + 8)
                    v = here[half]
                    high, side = kz[z, at], ky[z, at]
                    total = across[half] + (high * above[half] + flow[half] * below[half])
                    total = total + (side * pltpu.roll(v, 127, 1) + pltpu.roll(side * v, 1, 1))
                    total = total - diag[z, at] * v
                    if sweep == 0:
                        right = v + (heat[z, at] + heated * cavity[z, at])
                        rhs[z, at] = right
                        new[z, at] = v + (total + right) * (1.0 / cheb_center)
                    else:
                        a, b = pairs[sweep - 1]
                        new[z, at] = v + (a * (v - new[z, at]) + b * (total + rhs[z, at]))
                    next_flow.append(high)
                below, here, flow = here, above, tuple(next_flow)
            return below, here, flow

        def row_of(ref, z):
            return (ref[z, 0:8], ref[z, 8:16])

        lax.fori_loop(
            0, trips, rows, (row_of(now, begin - 1), row_of(now, begin), row_of(kz, begin - 1))
        )

    for step in range(STEPS):
        for sweep in range(SWEEPS):
            now, new = (xa, xb) if sweep % 2 == 0 else (xb, xa)
            apply(new, now, step, sweep)

    for z in range(ROWS):
        for half in range(2):
            at = slice(8 * half, 8 * half + 8)
            v = xa[HALO + z, at]
            if z < 24:
                side = pltpu.roll(xa[HALO + 40 + z % 8, at], 96 - 32 * (z // 8), 1)
            else:
                side = 0.0
            out[pl.ds(half * ROWS + z, 8, stride=2 * ROWS), :] = jnp.where(lane < YB, v, side)


def cycle_kernel(place, offsets, cells, base, out):
    b = place[4]
    for i in range(5):
        at = slice(8 * i, 8 * i + 8)
        ids, lump = cells[b, at], base[b, at]
        fixed = ids > 0
        spots = jnp.where(fixed, ids + (YB - 1), 0)
        gains, shifts = [], []
        gain, shift = jnp.ones((8, 128), jnp.float32), jnp.zeros((8, 128), jnp.float32)
        for g in range(NT):
            rate = jnp.where(fixed, lookup(offsets[g, 24:25, :], spots), 0.0)
            m, o = 1.0 / (lump + rate), offsets[g, at]
            gains.append(m)
            shifts.append(o)
            gain, shift = m * gain, m * shift + o
        value = shift / (1.0 - gain)
        for g in range(NT):
            out[g, at] = value
            value = gains[g] * value + shifts[g]


def unpack_kernel(folded, out):
    for by in range(2):
        parts = []
        for bz in range(8):
            parts = parts + unfold(folded[by * 8 + bz])
        whole = jnp.concatenate(parts, axis=0).T
        out[YB * by : YB * by + YB, :] = whole[0:YB]


def call(kernel, outs, n_in, n_smem, scratch=(), flops=0, nbytes=0):
    vmem = pl.BlockSpec(memory_space=pltpu.VMEM)
    smem = pl.BlockSpec(memory_space=pltpu.SMEM)
    return pl.pallas_call(
        kernel,
        out_shape=outs,
        in_specs=[smem] * n_smem + [vmem] * n_in,
        out_specs=jax.tree.map(lambda _: vmem, outs),
        scratch_shapes=list(scratch),
        compiler_params=pltpu.CompilerParams(vmem_limit_bytes=40 * 1024 * 1024),
        cost_estimate=pl.CostEstimate(flops=flops, bytes_accessed=nbytes, transcendentals=0),
    )


def f32(*shape):
    return jax.ShapeDtypeStruct(shape, jnp.float32)


def per_device(start_guess, material, channel, coolant_temp, htc_index, htc_levels, melt_steps):
    tm, sp = lax.axis_index("tm"), lax.axis_index("space")
    place = jnp.stack([tm % 2, sp % 8, sp // 8, melt_steps[0], tm]).astype(jnp.int32)
    packed, scaled, cells, base, tables = call(
        pack_kernel,
        (
            f32(16, 2, ZB, 128),
            f32(16, ROWS, 128),
            jax.ShapeDtypeStruct((16, ROWS, 128), jnp.int32),
            f32(16, ROWS, 128),
            f32(8, 128),
        ),
        5,
        2,
        scratch=[pltpu.VMEM((8, 128), jnp.int32)],
        nbytes=4000000,
    )(place, htc_levels, start_guess[0, 0], material[0], channel[0], coolant_temp, htc_index)

    received = lax.all_to_all(packed, "space", 0, 0, tiled=True)

    lower = [(8 * h + i, 8 * h + i + 1) for h in range(2) for i in range(7)]
    upper = [(d, s) for s, d in lower]
    swap = [(i, i ^ 1) for i in range(NT)]
    top, bottom = received[:, :, 0:HALO], received[:, :, HALO:ZB]
    other = lax.ppermute(received[:, 1], "tm", swap)
    up_mc = lax.ppermute(bottom[:, 1], "space", lower)
    down_mc = lax.ppermute(top[:, 1], "space", upper)
    up = lax.ppermute(bottom[:, 0], "space", lower)
    down = lax.ppermute(top[:, 0], "space", upper)
    other_up = lax.ppermute(up_mc, "tm", swap)
    other_down = lax.ppermute(down_mc, "tm", swap)

    flat = lambda v: v.reshape(-1, 128)
    big = pltpu.VMEM((ZE + 8, 16, 128), jnp.float32)
    fine = call(
        fine_kernel,
        f32(16 * ROWS, 128),
        9,
        1,
        scratch=[big] * 10,
        flops=70000000,
        nbytes=4000000,
    )(
        place, flat(received), flat(up), flat(down), flat(up_mc), flat(down_mc),
        flat(other), flat(other_up), flat(other_down), tables,
    )
    fine = lax.all_to_all(fine.reshape(16, ROWS, 128), "space", 0, 0, tiled=True)

    offsets = lax.all_to_all(fine - scaled, "tm", 0, 0, tiled=True)
    starts = call(cycle_kernel, f32(16, ROWS, 128), 3, 1, nbytes=2000000)(
        place, offsets, cells, base
    )
    starts = lax.all_to_all(starts, "tm", 0, 0, tiled=True)
    unpack = call(unpack_kernel, f32(CY, CZ), 1, 0, nbytes=1000000)
    return unpack(starts)[None, None], unpack(fine)[None, None]


def solution(mesh):
    return jax.shard_map(
        per_device,
        mesh=mesh,
        in_specs=(
            P("tm", "space", None, None),
            P("space", None, None),
            P("space", None, None),
            P("tm", None),
            P("tm", None),
            P(),
            P("tm"),
        ),
        out_specs=(P("tm", "space", None, None), P("tm", "space", None, None)),
        check_vma=False,
    )
```

```python
import jax
import jax.numpy as jnp
from jax import lax
from jax.experimental import pallas as pl
from jax.experimental.pallas import tpu as pltpu
from jax.sharding import PartitionSpec as P

NT = 16
NX = 16
CY = 192
CZ = 384
STEPS = 4
SWEEPS = 6
SEGS = 32
LEVELS = 16

time_step = 0.25
melt_rate = 4.0
lam_high = 1.0 + time_step * (12.0 * 3.0 + 8.0)
cheb_center = 0.5 * (lam_high + 1.0)
cheb_half = 0.5 * (lam_high - 1.0)
cheb_ratio = cheb_center / cheb_half
lump_rate = 0.1 / NT

ZB = 48
HALO = STEPS * SWEEPS
ZE = ZB + 2 * HALO
YB = 96
ROWS = 40
UNROLL = 96


def chebyshev():
    rho = 1.0 / cheb_ratio
    pairs = []
    for _ in range(SWEEPS - 1):
        rho_next = 1.0 / (2.0 * cheb_ratio - rho)
        pairs.append((rho_next * rho, 2.0 * rho_next / cheb_half))
        rho = rho_next
    return pairs


def lanes(rows):
    return lax.broadcasted_iota(jnp.int32, (rows, 128), 1)


def lookup(row, index):
    return jnp.take_along_axis(jnp.broadcast_to(row, index.shape), index, axis=1, mode="promise_in_bounds")


def conductivity(material):
    return jnp.where(material == 0.0, 1.0, jnp.where(material == 1.0, 3.0, 0.6)).astype(jnp.float32)


def window(plane, by):
    part = plane[64 * by : 64 * by + 128, :].T
    return part if by == 0 else pltpu.roll(part, 96, 1)


def fold(block):
    tail = block[40:48]
    side = [pltpu.roll(tail, 96, 1), pltpu.roll(tail, 64, 1), pltpu.roll(tail, 32, 1)]
    side = side + [jnp.zeros((8, 128), jnp.float32)] * 2
    lane = lanes(8)
    return [jnp.where(lane < YB, block[8 * i : 8 * i + 8], side[i]) for i in range(5)]


def unfold(folded):
    lane = lanes(8)
    tail = jnp.where(
        lane < 32,
        pltpu.roll(folded[0:8], 32, 1),
        jnp.where(lane < 64, pltpu.roll(folded[8:16], 64, 1), pltpu.roll(folded[16:24], 96, 1)),
    )
    return [folded[8 * i : 8 * i + 8] for i in range(5)] + [tail]


def pack_kernel(
    start, material, channel, coolant, index, levels, packed, rest, tables, fields, labels, small, ids, sems
):
    copies = [
        pltpu.make_async_copy(channel, labels.at[0], sems.at[0]),
        pltpu.make_async_copy(material, labels.at[1], sems.at[1]),
        pltpu.make_async_copy(start, fields, sems.at[2]),
        pltpu.make_async_copy(index, ids, sems.at[3]),
        pltpu.make_async_copy(coolant, small.at[0:1], sems.at[4]),
        pltpu.make_async_copy(levels, small.at[1:2], sems.at[5]),
    ]
    for copy in copies:
        copy.start()
    core = lax.rem(lax.axis_index("tm"), 2)
    tables[...] = jnp.zeros_like(tables)
    copies[0].wait()
    seg = [window(labels[0].astype(jnp.float32), by) for by in range(2)]
    copies[1].wait()
    mat = [window(labels[1].astype(jnp.float32), by) for by in range(2)]
    copies[2].wait()
    field = [window(fields[...], by) for by in range(2)]
    for by in range(2):
        mine = jnp.where(core == 0, mat[by], seg[by])
        theirs = jnp.where(core == 0, seg[by], mat[by])
        for bz in range(8):
            at = slice(ZB * bz, ZB * bz + ZB)
            packed[8 * by + bz, 0] = field[by][at]
            packed[8 * by + bz, 1] = mine[at]
            rest[8 * by + bz] = theirs[at]
    for copy in copies[3:]:
        copy.wait()
    tables[0:1, 0:LEVELS] = small[1:2, 0:LEVELS]
    tables[1:2, 0:SEGS] = small[0:1, 0:SEGS]
    tables[2:3, 0:SEGS] = ids[...].astype(jnp.float32)
    which = tables[2:3, :].astype(jnp.int32)
    levels_row = tables[0:1, :]
    picked = jnp.zeros((1, 128), jnp.float32)
    for level in range(LEVELS):
        picked = jnp.where(which == level, levels_row[:, level : level + 1], picked)
    picked = jnp.where(lanes(1) < SEGS, picked, 0.0)
    heat = picked * tables[1:2, :]
    tables[0:1, :] = pltpu.roll(picked, 1, 1)
    tables[1:2, :] = pltpu.roll(heat, 1, 1)
    tables[2:3, :] = pltpu.roll(picked, YB, 1)


def coarse_kernel(packed, rest, tables, scaled, cells, base):
    core = lax.rem(lax.axis_index("tm"), 2)
    rate_table = tables[0:1, :]
    negated = -tables[2:3, :]
    lane = lanes(8)
    sub = lax.broadcasted_iota(jnp.int32, (8, 128), 0)

    def block(b, carry):
        mine, theirs = packed[b, 1], rest[b]
        f = fold(packed[b, 0])
        m = fold(jnp.where(core == 0, mine, theirs))
        s = fold(jnp.where(core == 0, theirs, mine))
        for i in range(5):
            ids = s[i].astype(jnp.int32)
            lump = 1.0 + lump_rate * conductivity(m[i])
            value = f[i] / (lump + lookup(rate_table, ids))
            if i == 3:
                value = jnp.where((sub == 0) & (lane >= YB), negated, value)
            scaled[b, 8 * i : 8 * i + 8] = value
            cells[b, 8 * i : 8 * i + 8] = ids
            base[b, 8 * i : 8 * i + 8] = lump
        return carry

    lax.fori_loop(0, 16, block, 0, unroll=4)


def strided(ref, pitch, at, half):
    return ref[pl.ds(half * pitch + at, 8, stride=2 * pitch), :]


def operator_kernel(
    received, up, down, other, other_up, other_down, tables, kz, ky, kx, grow, heat, cavity, cond, rate,
):
    core = lax.rem(lax.axis_index("tm"), 2)
    bz, by = lax.rem(lax.axis_index("space"), 8), lax.div(lax.axis_index("space"), 8)
    lane = lanes(8)
    sub = lax.broadcasted_iota(jnp.int32, (8, 128), 0)
    rate_table = tables[0:1, :]
    heat_table = tables[1:2, :]

    for z in range(ZE):
        for half in range(2):
            to = slice(8 * half, 8 * half + 8)
            if z < HALO:
                a, b = strided(up, HALO, z, half), strided(other_up, HALO, z, half)
            elif z < HALO + ZB:
                a = strided(received, 2 * ZB, z - HALO + ZB, half)
                b = strided(other, ZB, z - HALO, half)
            else:
                a = strided(down, HALO, z - HALO - ZB, half)
                b = strided(other_down, HALO, z - HALO - ZB, half)
            mat = jnp.where(core == 0, a, b)
            seg = jnp.where(core == 0, b, a).astype(jnp.int32)
            cond[z, to] = conductivity(mat)
            cavity[z, to] = jnp.where(mat == 2.0, time_step * melt_rate, 0.0)
            heat[z, to] = time_step * lookup(heat_table, seg)
            rate[z, to] = 1.0 + time_step * lookup(rate_table, seg)

    last = jnp.where(by == 0, 127, YB - 1)
    first = jnp.where(by == 0, 0, YB)
    y_inner = jnp.where(lane == last, 0.0, 0.5 * time_step)
    y_edge = jnp.where((lane == last) | (lane == first), time_step, 0.0)
    x_inner = jnp.where(sub == 7, 0.0, 0.5 * time_step)
    edges = (jnp.where(sub == 0, time_step, 0.0), jnp.where(sub == 7, time_step, 0.0))
    z0 = bz * ZB - HALO
    pairs = chebyshev()
    flow = [jnp.zeros((8, 128), jnp.float32)] * 2
    for z in range(ZE - 1):
        gz = z + z0
        inner = jnp.where((gz == -1) | (gz == CZ - 1), 0.0, 0.5 * time_step)
        z_edge = jnp.where((gz == 0) | (gz == CZ - 1), time_step, 0.0)
        even, odd = cond[z, 0:8], cond[z, 8:16]
        between = (0.5 * time_step) * (even + odd)
        beyond = x_inner * (odd + pltpu.roll(even, 7, 0))
        kx[z, 0:8] = between
        kx[z, 8:16] = beyond
        across = (between + pltpu.roll(beyond, 1, 0), between + beyond)
        for half in range(2):
            at = slice(8 * half, 8 * half + 8)
            c = (even, odd)[half]
            high = inner * (c + cond[z + 1, at])
            kz[z, at] = high
            side = y_inner * (c + pltpu.roll(c, 127, 1))
            ky[z, at] = side
            total = across[half] + side + pltpu.roll(side, 1, 1) + high + flow[half]
            total = total + c * (edges[half] + y_edge + z_edge)
            diag = rate[z, at] + total
            grow[0, z, at] = 1.0 + (1.0 - diag) * (1.0 / cheb_center)
            for sweep, (a, b) in enumerate(pairs):
                grow[sweep + 1, z, at] = (1.0 + a) - b * diag
            flow[half] = high


def fine_kernel(melt, received, up, down, kz, ky, kx, grow, heat, cavity, out, xa, xb, rhs):
    lane = lanes(8)
    for z in range(ZE):
        for half in range(2):
            to = slice(8 * half, 8 * half + 8)
            if z < HALO:
                xa[z, to] = strided(up, HALO, z, half)
            elif z < HALO + ZB:
                xa[z, to] = strided(received, 2 * ZB, z - HALO, half)
            else:
                xa[z, to] = strided(down, HALO, z - HALO - ZB, half)

    pairs = chebyshev()

    def apply(new, now, step, sweep):
        j = step * SWEEPS + sweep
        begin, count = j + 1, ZE - 2 - 2 * j
        trips = -(-count // UNROLL)
        unroll = -(-count // trips)
        heated = jnp.where(step < melt[0], 1.0, 0.0)

        def rows(i, carry):
            below, here, flow = carry
            base = begin + i * unroll
            xs = [below, here]
            for u in range(unroll):
                xs.append((now[base + u + 1, 0:8], now[base + u + 1, 8:16]))
            flows = [flow]
            loaded = []
            for u in range(unroll):
                z = base + u
                row = []
                for half in range(2):
                    at = slice(8 * half, 8 * half + 8)
                    if sweep == 0:
                        two = (heat[z, at], cavity[z, at])
                    else:
                        two = (new[z, at], rhs[z, at])
                    row.append((kz[z, at], ky[z, at], kx[z, at], grow[sweep, z, at]) + two)
                flows.append((row[0][0], row[1][0]))
                loaded.append(row)
            results = []
            for u in range(unroll):
                z = base + u
                even, odd = xs[u + 1]
                between, beyond = loaded[u][0][2], loaded[u][1][2]
                across = (
                    between * odd + pltpu.roll(beyond * odd, 1, 0),
                    between * even + beyond * pltpu.roll(even, 7, 0),
                )
                for half in range(2):
                    at = slice(8 * half, 8 * half + 8)
                    v = xs[u + 1][half]
                    high, side, _, keep, p, q = loaded[u][half]
                    total = across[half] + (high * xs[u + 2][half] + flows[u][half] * xs[u][half])
                    total = total + (side * pltpu.roll(v, 127, 1) + pltpu.roll(side * v, 1, 1))
                    if sweep == 0:
                        source = p + heated * q
                        results.append((rhs, z, at, v + source))
                        results.append((new, z, at, keep * v + (total + source) * (1.0 / cheb_center)))
                    else:
                        a, b = pairs[sweep - 1]
                        results.append((new, z, at, (keep * v - a * p) + b * (total + q)))
            for ref, z, at, value in results:
                ref[z, at] = value
            return xs[unroll], xs[unroll + 1], flows[unroll]

        def row_of(ref, z):
            return (ref[z, 0:8], ref[z, 8:16])

        state = (row_of(now, begin - 1), row_of(now, begin), row_of(kz, begin - 1))
        if trips == 1:
            rows(0, state)
        else:
            lax.fori_loop(0, trips, rows, state)

    for step in range(STEPS):
        for sweep in range(SWEEPS):
            now, new = (xa, xb) if sweep % 2 == 0 else (xb, xa)
            apply(new, now, step, sweep)

    for z in range(ROWS):
        for half in range(2):
            at = slice(8 * half, 8 * half + 8)
            v = xa[HALO + z, at]
            if z < 24:
                side = pltpu.roll(xa[HALO + 40 + z % 8, at], 96 - 32 * (z // 8), 1)
            else:
                side = 0.0
            out[pl.ds(half * ROWS + z, 8, stride=2 * ROWS), :] = jnp.where(lane < YB, v, side)


def cycle_kernel(offsets, cells, base, out):
    b = lax.axis_index("tm")
    tiles = range(5)
    ids = [cells[b, 8 * i : 8 * i + 8] for i in tiles]
    lump = [base[b, 8 * i : 8 * i + 8] for i in tiles]
    fixed = [v > 0 for v in ids]
    spots = [jnp.where(fixed[i], ids[i] + (YB - 1), 0) for i in tiles]
    gain = [jnp.ones((8, 128), jnp.float32)] * 5
    shift = [jnp.zeros((8, 128), jnp.float32)] * 5
    gains = []
    for g in range(NT):
        table = offsets[g, 24:25, :]
        row = [
            1.0 / (lump[i] + jnp.where(fixed[i], lookup(table, spots[i]), 0.0)) for i in tiles
        ]
        gains.append(row)
        for i in tiles:
            gain[i] = row[i] * gain[i]
            shift[i] = row[i] * shift[i] + offsets[g, 8 * i : 8 * i + 8]
    value = [shift[i] / (1.0 - gain[i]) for i in tiles]
    for g in range(NT):
        for i in tiles:
            out[g, 8 * i : 8 * i + 8] = value[i]
            value[i] = gains[g][i] * value[i] + offsets[g, 8 * i : 8 * i + 8]


def unpack_kernel(folded, out):
    for by in range(2):
        parts = []
        for bz in range(8):
            parts = parts + unfold(folded[by * 8 + bz])
        whole = jnp.concatenate(parts, axis=0).T
        out[YB * by : YB * by + YB, :] = whole[0:YB]


VMEM = pl.BlockSpec(memory_space=pltpu.VMEM)
SMEM = pl.BlockSpec(memory_space=pltpu.SMEM)
HBM = pl.BlockSpec(memory_space=pl.ANY)


def call(kernel, outs, in_specs, scratch=(), limit=8, flops=0, nbytes=0):
    return pl.pallas_call(
        kernel,
        out_shape=outs,
        in_specs=in_specs,
        out_specs=jax.tree.map(lambda _: VMEM, outs),
        scratch_shapes=list(scratch),
        compiler_params=pltpu.CompilerParams(vmem_limit_bytes=limit * 1024 * 1024),
        cost_estimate=pl.CostEstimate(flops=flops, bytes_accessed=nbytes, transcendentals=0),
    )


def f32(*shape):
    return jax.ShapeDtypeStruct(shape, jnp.float32)


def i32(*shape):
    return jax.ShapeDtypeStruct(shape, jnp.int32)


def per_device(start_guess, material, channel, coolant_temp, htc_index, htc_levels, melt_steps):
    packed, rest, tables = call(
        pack_kernel,
        (f32(16, 2, ZB, 128), f32(16, ZB, 128), f32(8, 128)),
        [HBM] * 6,
        scratch=[
            pltpu.VMEM((CY, CZ), jnp.float32),
            pltpu.VMEM((2, CY, CZ), jnp.int32),
            pltpu.VMEM((8, SEGS), jnp.float32),
            pltpu.VMEM((1, SEGS), jnp.int32),
            pltpu.SemaphoreType.DMA((6,)),
        ],
        nbytes=4000000,
    )(
        start_guess[0, 0],
        material[0],
        channel[0],
        coolant_temp,
        htc_index,
        jnp.pad(htc_levels, (0, SEGS - LEVELS))[None],
    )

    received = lax.all_to_all(packed, "space", 0, 0, tiled=True)

    lower = [(8 * h + i, 8 * h + i + 1) for h in range(2) for i in range(7)]
    upper = [(d, s) for s, d in lower]
    swap = [(i, i ^ 1) for i in range(NT)]
    top, bottom = received[:, :, 0:HALO], received[:, :, HALO:ZB]
    other = lax.ppermute(received[:, 1], "tm", swap)
    up_mc = lax.ppermute(bottom[:, 1], "space", lower)
    down_mc = lax.ppermute(top[:, 1], "space", upper)
    up = lax.ppermute(bottom[:, 0], "space", lower)
    down = lax.ppermute(top[:, 0], "space", upper)
    other_up = lax.ppermute(up_mc, "tm", swap)
    other_down = lax.ppermute(down_mc, "tm", swap)

    flat = lambda v: v.reshape(-1, 128)
    plane = f32(ZE, 16, 128)
    received = flat(received)
    operator = call(
        operator_kernel,
        (plane, plane, plane, f32(SWEEPS, ZE, 16, 128), plane, plane),
        [VMEM] * 7,
        scratch=[pltpu.VMEM(plane.shape, jnp.float32)] * 2,
        flops=10000000,
        nbytes=8000000,
    )(
        received, flat(up_mc), flat(down_mc), flat(other), flat(other_up), flat(other_down), tables
    )
    scaled, cells, base = call(
        coarse_kernel,
        (f32(16, ROWS, 128), i32(16, ROWS, 128), f32(16, ROWS, 128)),
        [VMEM] * 3,
        nbytes=2000000,
    )(packed, rest, tables)
    fine = call(
        fine_kernel,
        f32(16 * ROWS, 128),
        [SMEM] + [VMEM] * 9,
        scratch=[pltpu.VMEM((ZE + 2, 16, 128), jnp.float32)] * 3,
        flops=70000000,
        nbytes=4000000,
    )(melt_steps, received, flat(up), flat(down), *operator)
    fine = lax.all_to_all(fine.reshape(16, ROWS, 128), "space", 0, 0, tiled=True)

    offsets = lax.all_to_all(fine - scaled, "tm", 0, 0, tiled=True)
    starts = call(cycle_kernel, f32(16, ROWS, 128), [VMEM] * 3, nbytes=2000000)(
        offsets, cells, base
    )
    starts = lax.all_to_all(starts, "tm", 0, 0, tiled=True)
    unpack = call(unpack_kernel, f32(CY, CZ), [VMEM], nbytes=1000000)
    return unpack(starts)[None, None], unpack(fine)[None, None]


def solution(mesh):
    return jax.shard_map(
        per_device,
        mesh=mesh,
        in_specs=(
            P("tm", "space", None, None),
            P("space", None, None),
            P("space", None, None),
            P("tm", None),
            P("tm", None),
            P(),
            P("tm"),
        ),
        out_specs=(P("tm", "space", None, None), P("tm", "space", None, None)),
        check_vma=False,
    )
```

```python
import jax
import jax.numpy as jnp
from jax import lax
from jax.experimental import pallas as pl
from jax.experimental.pallas import tpu as pltpu
from jax.sharding import PartitionSpec as P

NT = 16
NX = 16
CY = 192
CZ = 384
STEPS = 4
SWEEPS = 6
SEGS = 32
LEVELS = 16

time_step = 0.25
melt_rate = 4.0
lam_high = 1.0 + time_step * (12.0 * 3.0 + 8.0)
cheb_center = 0.5 * (lam_high + 1.0)
cheb_half = 0.5 * (lam_high - 1.0)
cheb_ratio = cheb_center / cheb_half
lump_rate = 0.1 / NT

ZB = 48
HALO = STEPS * SWEEPS
ZE = ZB + 2 * HALO
YB = 96
ROWS = 40
EARLY = 12
LIMIT = 60


def chebyshev():
    rho = 1.0 / cheb_ratio
    pairs = []
    for _ in range(SWEEPS - 1):
        rho_next = 1.0 / (2.0 * cheb_ratio - rho)
        pairs.append((rho_next * rho, 2.0 * rho_next / cheb_half))
        rho = rho_next
    return pairs


def lanes(rows):
    return lax.broadcasted_iota(jnp.int32, (rows, 128), 1)


def lookup(row, index):
    return jnp.take_along_axis(jnp.broadcast_to(row, index.shape), index, axis=1, mode="promise_in_bounds")


def conductivity(material):
    return jnp.where(material == 0.0, 1.0, jnp.where(material == 1.0, 3.0, 0.6)).astype(jnp.float32)


def window(plane, by):
    part = plane[64 * by : 64 * by + 128, :].T
    return part if by == 0 else pltpu.roll(part, 96, 1)


def fold(block):
    tail = block[40:48]
    side = [pltpu.roll(tail, 96, 1), pltpu.roll(tail, 64, 1), pltpu.roll(tail, 32, 1)]
    side = side + [jnp.zeros((8, 128), jnp.float32)] * 2
    lane = lanes(8)
    return [jnp.where(lane < YB, block[8 * i : 8 * i + 8], side[i]) for i in range(5)]


def unfold(folded):
    lane = lanes(8)
    tail = jnp.where(
        lane < 32,
        pltpu.roll(folded[0:8], 32, 1),
        jnp.where(lane < 64, pltpu.roll(folded[8:16], 64, 1), pltpu.roll(folded[16:24], 96, 1)),
    )
    return [folded[8 * i : 8 * i + 8] for i in range(5)] + [tail]


def pack_kernel(
    start, material, channel, coolant, index, levels, packed, rest, tables, fields, labels, small, ids, steps, sems
):
    copies = [
        pltpu.make_async_copy(channel, labels.at[0], sems.at[0]),
        pltpu.make_async_copy(material, labels.at[1], sems.at[1]),
        pltpu.make_async_copy(start, fields, sems.at[2]),
        pltpu.make_async_copy(index, ids, sems.at[3]),
        pltpu.make_async_copy(coolant, small, sems.at[4]),
        pltpu.make_async_copy(levels, steps, sems.at[5]),
    ]
    for copy in copies:
        copy.start()
    core = lax.rem(lax.axis_index("tm"), 2)
    tables[...] = jnp.zeros_like(tables)
    copies[0].wait()
    seg = [window(labels[0].astype(jnp.float32), by) for by in range(2)]
    copies[1].wait()
    mat = [window(labels[1].astype(jnp.float32), by) for by in range(2)]
    copies[2].wait()
    field = [window(fields[...], by) for by in range(2)]
    for by in range(2):
        mine = jnp.where(core == 0, mat[by], seg[by])
        theirs = jnp.where(core == 0, seg[by], mat[by])
        for bz in range(8):
            at = slice(ZB * bz, ZB * bz + ZB)
            packed[8 * by + bz, 0] = field[by][at]
            packed[8 * by + bz, 1] = mine[at]
            rest[8 * by + bz] = theirs[at]
    for copy in copies[3:]:
        copy.wait()
    tables[1:2, 0:SEGS] = small[...]
    tables[2:3, 0:SEGS] = ids[...].astype(jnp.float32)
    which = tables[2:3, :].astype(jnp.int32)
    picked = jnp.zeros((1, 128), jnp.float32)
    for level in range(LEVELS):
        picked = jnp.where(which == level, steps[level], picked)
    picked = jnp.where(lanes(1) < SEGS, picked, 0.0)
    heat = picked * tables[1:2, :]
    tables[0:1, :] = pltpu.roll(picked, 1, 1)
    tables[1:2, :] = pltpu.roll(heat, 1, 1)
    tables[2:3, :] = pltpu.roll(picked, YB, 1)


def coarse_kernel(packed, rest, tables, scaled, cells, base):
    core = lax.rem(lax.axis_index("tm"), 2)
    rate_table = tables[0:1, :]
    negated = -tables[2:3, :]
    lane = lanes(8)
    sub = lax.broadcasted_iota(jnp.int32, (8, 128), 0)

    def block(b, carry):
        mine, theirs = packed[b, 1], rest[b]
        f = fold(packed[b, 0])
        m = fold(jnp.where(core == 0, mine, theirs))
        s = fold(jnp.where(core == 0, theirs, mine))
        for i in range(5):
            ids = s[i].astype(jnp.int32)
            lump = 1.0 + lump_rate * conductivity(m[i])
            value = f[i] / (lump + lookup(rate_table, ids))
            if i == 3:
                value = jnp.where((sub == 0) & (lane >= YB), negated, value)
            scaled[b, 8 * i : 8 * i + 8] = value
            cells[b, 8 * i : 8 * i + 8] = ids
            base[b, 8 * i : 8 * i + 8] = lump
        return carry

    lax.fori_loop(0, 16, block, 0, unroll=4)


def strided(ref, pitch, at, half):
    return ref[pl.ds(half * pitch + at, 8, stride=2 * pitch), :]


def operator_rows(refs, spans, load, tables):
    cond, rate, kz, ky, kx, grow, heat, cavity = refs
    core = lax.rem(lax.axis_index("tm"), 2)
    bz, by = lax.rem(lax.axis_index("space"), 8), lax.div(lax.axis_index("space"), 8)
    lane = lanes(8)
    sub = lax.broadcasted_iota(jnp.int32, (8, 128), 0)
    rate_table = tables[0:1, :]
    heat_table = tables[1:2, :]

    for fresh, _, _ in spans:
        for z in fresh:
            for half in range(2):
                to = slice(8 * half, 8 * half + 8)
                a, b = load(z, half)
                mat = jnp.where(core == 0, a, b)
                seg = jnp.where(core == 0, b, a).astype(jnp.int32)
                cond[z, to] = conductivity(mat)
                cavity[z, to] = jnp.where(mat == 2.0, time_step * melt_rate, 0.0)
                heat[z, to] = time_step * lookup(heat_table, seg)
                rate[z, to] = 1.0 + time_step * lookup(rate_table, seg)

    last = jnp.where(by == 0, 127, YB - 1)
    first = jnp.where(by == 0, 0, YB)
    y_inner = jnp.where(lane == last, 0.0, 0.5 * time_step)
    y_edge = jnp.where((lane == last) | (lane == first), time_step, 0.0)
    x_inner = jnp.where(sub == 7, 0.0, 0.5 * time_step)
    edges = (jnp.where(sub == 0, time_step, 0.0), jnp.where(sub == 7, time_step, 0.0))
    z0 = bz * ZB - HALO
    pairs = chebyshev()
    for _, faces, before in spans:
        flow = [None, None] if before is None else [kz[before, 0:8], kz[before, 8:16]]
        for z in faces:
            gz = z + z0
            inner = jnp.where((gz == -1) | (gz == CZ - 1), 0.0, 0.5 * time_step)
            z_edge = jnp.where((gz == 0) | (gz == CZ - 1), time_step, 0.0)
            even, odd = cond[z, 0:8], cond[z, 8:16]
            between = (0.5 * time_step) * (even + odd)
            beyond = x_inner * (odd + pltpu.roll(even, 7, 0))
            kx[z, 0:8] = between
            kx[z, 8:16] = beyond
            across = (between + pltpu.roll(beyond, 1, 0), between + beyond)
            for half in range(2):
                at = slice(8 * half, 8 * half + 8)
                c = (even, odd)[half]
                high = inner * (c + cond[z + 1, at])
                kz[z, at] = high
                side = y_inner * (c + pltpu.roll(c, 127, 1))
                ky[z, at] = side
                if flow[half] is not None:
                    total = across[half] + side + pltpu.roll(side, 1, 1) + high + flow[half]
                    total = total + c * (edges[half] + y_edge + z_edge)
                    diag = rate[z, at] + total
                    grow[0, z, at] = 1.0 + (1.0 - diag) * (1.0 / cheb_center)
                    for sweep, (a, b) in enumerate(pairs):
                        grow[sweep + 1, z, at] = (1.0 + a) - b * diag
                flow[half] = high


def operator_core_kernel(received, other, tables, *refs):
    def load(z, half):
        z = z - HALO
        return strided(received, 2 * ZB, z + ZB, half), strided(other, ZB, z, half)

    spans = [(range(HALO, HALO + ZB), range(HALO, HALO + ZB - 1), None)]
    operator_rows(refs, spans, load, tables)


def operator_rim_kernel(up, down, other, tables, *refs):
    def load(z, half):
        if z < HALO:
            return strided(up, HALO, 16 * HALO + z, half), strided(other, HALO, z, half)
        z = z - HALO - ZB
        at = 16 * HALO + z
        return strided(down, HALO, at, half), strided(other, HALO, at, half)

    ends = HALO + ZB
    spans = [(range(0, HALO), range(0, HALO + 1), None), (range(ends, ZE), range(ends - 1, ZE - 1), ends - 2)]
    operator_rows(refs[8:], spans, load, tables)


def sweep_rows(buffers, operator, heated, j, spans):
    xa, xb, rhs = buffers
    kz, ky, kx, grow, heat, cavity = operator
    pairs = chebyshev()
    sweep = j % SWEEPS
    now, new = (xa, xb) if j % 2 == 0 else (xb, xa)
    halves = [slice(0, 8), slice(8, 16)]
    results = []
    for begin, end in spans:
        xs = {z: [now[z, at] for at in halves] for z in range(begin - 1, end + 1)}
        flows = {z: [kz[z, at] for at in halves] for z in range(begin - 1, end)}
        for z in range(begin, end):
            even, odd = xs[z]
            between, beyond = kx[z, 0:8], kx[z, 8:16]
            across = (
                between * odd + pltpu.roll(beyond * odd, 1, 0),
                between * even + beyond * pltpu.roll(even, 7, 0),
            )
            for half, at in enumerate(halves):
                v, side, keep = xs[z][half], ky[z, at], grow[sweep, z, at]
                total = flows[z][half] * xs[z + 1][half] + flows[z - 1][half] * xs[z - 1][half]
                total = across[half] + total
                total = total + (side * pltpu.roll(v, 127, 1) + pltpu.roll(side * v, 1, 1))
                if sweep == 0:
                    source = heat[z, at] + heated * cavity[z, at]
                    results.append((rhs, z, at, v + source))
                    value = keep * v + (total + source) * (1.0 / cheb_center)
                else:
                    a, b = pairs[sweep - 1]
                    value = (keep * v - a * new[z, at]) + b * (total + rhs[z, at])
                results.append((new, z, at, value))
    for ref, z, at, value in results:
        ref[z, at] = value


def melting(melt, j):
    return jnp.where(j // SWEEPS < melt[0], 1.0, 0.0)


def fine_core_kernel(melt, received, kz, ky, kx, grow, heat, cavity, xa, xb, rhs):
    for z in range(ZB):
        xa[HALO + z, 0:8] = strided(received, 2 * ZB, z, 0)
        xa[HALO + z, 8:16] = strided(received, 2 * ZB, z, 1)
    for j in range(EARLY):
        spans = [(HALO + j + 1, HALO + ZB - j - 1)]
        sweep_rows((xa, xb, rhs), (kz, ky, kx, grow, heat, cavity), melting(melt, j), j, spans)


def fine_kernel(melt, up, down, kz, ky, kx, grow, heat, cavity, xa_in, xb_in, rhs_in, out, xa, xb, rhs):
    del xa_in, xb_in, rhs_in
    lane = lanes(8)
    for z in range(HALO):
        for half in range(2):
            at = slice(8 * half, 8 * half + 8)
            xa[z, at] = strided(up, HALO, z, half)
            xa[HALO + ZB + z, at] = strided(down, HALO, z, half)
    for j in range(HALO):
        spans = [(j + 1, ZE - 1 - j)]
        if j < EARLY:
            spans = [(j + 1, HALO + j + 1), (HALO + ZB - j - 1, ZE - 1 - j)]
        sweep_rows((xa, xb, rhs), (kz, ky, kx, grow, heat, cavity), melting(melt, j), j, spans)
    for z in range(ROWS):
        for half in range(2):
            at = slice(8 * half, 8 * half + 8)
            v = xa[HALO + z, at]
            if z < 24:
                side = pltpu.roll(xa[HALO + 40 + z % 8, at], 96 - 32 * (z // 8), 1)
            else:
                side = 0.0
            out[pl.ds(half * ROWS + z, 8, stride=2 * ROWS), :] = jnp.where(lane < YB, v, side)


def cycle_kernel(offsets, cells, base, out):
    b = lax.axis_index("tm")
    tiles = range(5)
    ids = [cells[b, 8 * i : 8 * i + 8] for i in tiles]
    lump = [base[b, 8 * i : 8 * i + 8] for i in tiles]
    fixed = [v > 0 for v in ids]
    spots = [jnp.where(fixed[i], ids[i] + (YB - 1), 0) for i in tiles]
    gain = [jnp.ones((8, 128), jnp.float32)] * 5
    shift = [jnp.zeros((8, 128), jnp.float32)] * 5
    gains = []
    for g in range(NT):
        table = offsets[g, 24:25, :]
        row = [
            1.0 / (lump[i] + jnp.where(fixed[i], lookup(table, spots[i]), 0.0)) for i in tiles
        ]
        gains.append(row)
        for i in tiles:
            gain[i] = row[i] * gain[i]
            shift[i] = row[i] * shift[i] + offsets[g, 8 * i : 8 * i + 8]
    value = [shift[i] / (1.0 - gain[i]) for i in tiles]
    for g in range(NT):
        for i in tiles:
            out[g, 8 * i : 8 * i + 8] = value[i]
            value[i] = gains[g][i] * value[i] + offsets[g, 8 * i : 8 * i + 8]


def unpack_kernel(folded, out):
    for by in range(2):
        parts = []
        for bz in range(8):
            parts = parts + unfold(folded[by * 8 + bz])
        whole = jnp.concatenate(parts, axis=0).T
        out[YB * by : YB * by + YB, :] = whole[0:YB]


VMEM = pl.BlockSpec(memory_space=pltpu.VMEM)
SMEM = pl.BlockSpec(memory_space=pltpu.SMEM)
HBM = pl.BlockSpec(memory_space=pl.ANY)


def call(kernel, outs, in_specs, scratch=(), limit=8, aliases={}, flops=0, nbytes=0):
    return pl.pallas_call(
        kernel,
        out_shape=outs,
        in_specs=in_specs,
        out_specs=jax.tree.map(lambda _: VMEM, outs),
        scratch_shapes=list(scratch),
        input_output_aliases=aliases,
        compiler_params=pltpu.CompilerParams(vmem_limit_bytes=limit * 1024 * 1024),
        cost_estimate=pl.CostEstimate(flops=flops, bytes_accessed=nbytes, transcendentals=0),
    )


def f32(*shape):
    return jax.ShapeDtypeStruct(shape, jnp.float32)


def i32(*shape):
    return jax.ShapeDtypeStruct(shape, jnp.int32)


def per_device(start_guess, material, channel, coolant_temp, htc_index, htc_levels, melt_steps):
    packed, rest, tables = call(
        pack_kernel,
        (f32(16, 2, ZB, 128), f32(16, ZB, 128), f32(8, 128)),
        [HBM] * 6,
        limit=LIMIT,
        scratch=[
            pltpu.VMEM((CY, CZ), jnp.float32),
            pltpu.VMEM((2, CY, CZ), jnp.int32),
            pltpu.VMEM((1, SEGS), jnp.float32),
            pltpu.VMEM((1, SEGS), jnp.int32),
            pltpu.SMEM((LEVELS,), jnp.float32),
            pltpu.SemaphoreType.DMA((6,)),
        ],
        nbytes=4000000,
    )(
        start_guess[0, 0],
        material[0],
        channel[0],
        coolant_temp,
        htc_index,
        htc_levels,
    )

    received = lax.all_to_all(packed, "space", 0, 0, tiled=True)

    lower = [(8 * h + i, 8 * h + i + 1) for h in range(2) for i in range(7)]
    upper = [(d, s) for s, d in lower]
    swap = [(i, i ^ 1) for i in range(NT)]
    other = lax.ppermute(received[:, 1], "tm", swap)
    both = lambda rows: jnp.stack([received[:, 0, rows], received[:, 1, rows]])
    up = lax.ppermute(both(slice(HALO, ZB)), "space", lower)
    down = lax.ppermute(both(slice(0, HALO)), "space", upper)

    flat = lambda v: v.reshape(-1, 128)
    plane = f32(ZE, 16, 128)
    planes = (plane,) * 5 + (f32(SWEEPS, ZE, 16, 128),) + (plane,) * 2
    received = flat(received)
    operator = call(operator_core_kernel, planes, [VMEM] * 3, flops=5000000, nbytes=4000000)(
        received, flat(other), tables
    )
    scaled, cells, base = call(
        coarse_kernel,
        (f32(16, ROWS, 128), i32(16, ROWS, 128), f32(16, ROWS, 128)),
        [VMEM] * 3,
        nbytes=2000000,
    )(packed, rest, tables)
    fields = call(
        fine_core_kernel, (plane,) * 3, [SMEM] + [VMEM] * 7, flops=20000000, nbytes=4000000
    )(melt_steps, received, *operator[2:])
    up, down, first = lax.optimization_barrier((up, down, fields[0]))
    fields = (first,) + tuple(fields[1:])
    other_rim = lax.ppermute(jnp.stack([up[1], down[1]]), "tm", swap)
    up, down = flat(up), flat(down)
    operator = call(
        operator_rim_kernel,
        planes,
        [VMEM] * 12,
        aliases={4 + i: i for i in range(8)},
        flops=5000000,
        nbytes=4000000,
    )(up, down, flat(other_rim), tables, *operator)
    fine, _, _, _ = call(
        fine_kernel,
        (f32(16 * ROWS, 128),) + (plane,) * 3,
        [SMEM] + [VMEM] * 11,
        aliases={9 + i: 1 + i for i in range(3)},
        flops=50000000,
        nbytes=4000000,
    )(melt_steps, up, down, *operator[2:], *fields)
    fine = lax.all_to_all(fine.reshape(16, ROWS, 128), "space", 0, 0, tiled=True)

    offsets = lax.all_to_all(fine - scaled, "tm", 0, 0, tiled=True)
    starts = call(cycle_kernel, f32(16, ROWS, 128), [VMEM] * 3, nbytes=2000000)(
        offsets, cells, base
    )
    starts = lax.all_to_all(starts, "tm", 0, 0, tiled=True)
    unpack = call(unpack_kernel, f32(CY, CZ), [VMEM], nbytes=1000000)
    return unpack(starts)[None, None], unpack(fine)[None, None]


def solution(mesh):
    return jax.shard_map(
        per_device,
        mesh=mesh,
        in_specs=(
            P("tm", "space", None, None),
            P("space", None, None),
            P("space", None, None),
            P("tm", None),
            P("tm", None),
            P(),
            P("tm"),
        ),
        out_specs=(P("tm", "space", None, None), P("tm", "space", None, None)),
        check_vma=False,
    )
```

```python
import jax
import jax.numpy as jnp
from jax import lax
from jax.experimental import pallas as pl
from jax.experimental.pallas import tpu as pltpu
from jax.sharding import PartitionSpec as P

NT = 16
NX = 16
CY = 192
CZ = 384
STEPS = 4
SWEEPS = 6
SEGS = 32
LEVELS = 16

time_step = 0.25
melt_rate = 4.0
lam_high = 1.0 + time_step * (12.0 * 3.0 + 8.0)
cheb_center = 0.5 * (lam_high + 1.0)
cheb_half = 0.5 * (lam_high - 1.0)
cheb_ratio = cheb_center / cheb_half
lump_rate = 0.1 / NT

ZB = 48
HALO = STEPS * SWEEPS
ZE = ZB + 2 * HALO
YB = 96
ROWS = 40
EARLY = 23
LIMIT = 60


def chebyshev():
    rho = 1.0 / cheb_ratio
    pairs = []
    for _ in range(SWEEPS - 1):
        rho_next = 1.0 / (2.0 * cheb_ratio - rho)
        pairs.append((rho_next * rho, 2.0 * rho_next / cheb_half))
        rho = rho_next
    return pairs


def lanes(rows):
    return lax.broadcasted_iota(jnp.int32, (rows, 128), 1)


def lookup(row, index):
    return jnp.take_along_axis(jnp.broadcast_to(row, index.shape), index, axis=1, mode="promise_in_bounds")


def conductivity(material):
    return jnp.where(material == 0.0, 1.0, jnp.where(material == 1.0, 3.0, 0.6)).astype(jnp.float32)


def window(plane, by):
    part = plane[64 * by : 64 * by + 128, :].T
    return part if by == 0 else pltpu.roll(part, 96, 1)


def fold(block):
    tail = block[40:48]
    side = [pltpu.roll(tail, 96, 1), pltpu.roll(tail, 64, 1), pltpu.roll(tail, 32, 1)]
    side = side + [jnp.zeros((8, 128), jnp.float32)] * 2
    lane = lanes(8)
    return [jnp.where(lane < YB, block[8 * i : 8 * i + 8], side[i]) for i in range(5)]


def unfold(folded):
    lane = lanes(8)
    tail = jnp.where(
        lane < 32,
        pltpu.roll(folded[0:8], 32, 1),
        jnp.where(lane < 64, pltpu.roll(folded[8:16], 64, 1), pltpu.roll(folded[16:24], 96, 1)),
    )
    return [folded[8 * i : 8 * i + 8] for i in range(5)] + [tail]


def pack_kernel(
    start, material, channel, coolant, index, levels, packed, rest, tables, fields, labels, small, ids, steps, sems
):
    copies = [
        pltpu.make_async_copy(channel, labels.at[0], sems.at[0]),
        pltpu.make_async_copy(material, labels.at[1], sems.at[1]),
        pltpu.make_async_copy(start, fields, sems.at[2]),
        pltpu.make_async_copy(index, ids, sems.at[3]),
        pltpu.make_async_copy(coolant, small, sems.at[4]),
        pltpu.make_async_copy(levels, steps, sems.at[5]),
    ]
    for copy in copies:
        copy.start()
    core = lax.axis_index("tm") & 1
    tables[...] = jnp.zeros_like(tables)
    copies[0].wait()
    seg = [window(labels[0].astype(jnp.float32), by) for by in range(2)]
    copies[1].wait()
    mat = [window(labels[1].astype(jnp.float32), by) for by in range(2)]
    copies[2].wait()
    field = [window(fields[...], by) for by in range(2)]
    for by in range(2):
        mine = jnp.where(core == 0, mat[by], seg[by])
        theirs = jnp.where(core == 0, seg[by], mat[by])
        for bz in range(8):
            at = slice(ZB * bz, ZB * bz + ZB)
            packed[8 * by + bz, 0] = field[by][at]
            packed[8 * by + bz, 1] = mine[at]
            rest[8 * by + bz] = theirs[at]
    for copy in copies[3:]:
        copy.wait()
    tables[1:2, 0:SEGS] = small[...]
    tables[2:3, 0:SEGS] = ids[...].astype(jnp.float32)
    which = tables[2:3, :].astype(jnp.int32)
    picked = jnp.zeros((1, 128), jnp.float32)
    for level in range(LEVELS):
        picked = jnp.where(which == level, steps[level], picked)
    picked = jnp.where(lanes(1) < SEGS, picked, 0.0)
    heat = picked * tables[1:2, :]
    tables[0:1, :] = pltpu.roll(picked, 1, 1)
    tables[1:2, :] = pltpu.roll(heat, 1, 1)
    tables[2:3, :] = pltpu.roll(picked, YB, 1)


def coarse_kernel(packed, rest, tables, scaled, cells, base):
    core = lax.axis_index("tm") & 1
    rate_table = tables[0:1, :]
    negated = -tables[2:3, :]
    lane = lanes(8)
    sub = lax.broadcasted_iota(jnp.int32, (8, 128), 0)

    def block(b, carry):
        mine, theirs = packed[b, 1], rest[b]
        f = fold(packed[b, 0])
        m = fold(jnp.where(core == 0, mine, theirs))
        s = fold(jnp.where(core == 0, theirs, mine))
        for i in range(5):
            ids = s[i].astype(jnp.int32)
            lump = 1.0 + lump_rate * conductivity(m[i])
            value = f[i] / (lump + lookup(rate_table, ids))
            if i == 3:
                value = jnp.where((sub == 0) & (lane >= YB), negated, value)
            scaled[b, 8 * i : 8 * i + 8] = value
            cells[b, 8 * i : 8 * i + 8] = ids
            base[b, 8 * i : 8 * i + 8] = lump
        return carry

    lax.fori_loop(0, 16, block, 0, unroll=4)


def strided(ref, pitch, at, half):
    return ref[pl.ds(half * pitch + at, 8, stride=2 * pitch), :]


def operator_rows(refs, spans, load, tables):
    cond, rate, kz, ky, kx, grow, heat, cavity = refs
    core = lax.axis_index("tm") & 1
    bz, by = lax.rem(lax.axis_index("space"), 8), lax.div(lax.axis_index("space"), 8)
    lane = lanes(8)
    sub = lax.broadcasted_iota(jnp.int32, (8, 128), 0)
    rate_table = tables[0:1, :]
    heat_table = tables[1:2, :]

    for fresh, _, _ in spans:
        for z in fresh:
            for half in range(2):
                to = slice(8 * half, 8 * half + 8)
                a, b = load(z, half)
                mat = jnp.where(core == 0, a, b)
                seg = jnp.where(core == 0, b, a).astype(jnp.int32)
                cond[z, to] = conductivity(mat)
                cavity[z, to] = jnp.where(mat == 2.0, time_step * melt_rate, 0.0)
                heat[z, to] = time_step * lookup(heat_table, seg)
                rate[z, to] = 1.0 + time_step * lookup(rate_table, seg)

    last = jnp.where(by == 0, 127, YB - 1)
    first = jnp.where(by == 0, 0, YB)
    y_inner = jnp.where(lane == last, 0.0, 0.5 * time_step)
    y_edge = jnp.where((lane == last) | (lane == first), time_step, 0.0)
    x_inner = jnp.where(sub == 7, 0.0, 0.5 * time_step)
    edges = (jnp.where(sub == 0, time_step, 0.0), jnp.where(sub == 7, time_step, 0.0))
    z0 = bz * ZB - HALO
    pairs = chebyshev()
    for _, faces, before in spans:
        flow = [None, None] if before is None else [kz[before, 0:8], kz[before, 8:16]]
        for z in faces:
            gz = z + z0
            inner = jnp.where((gz == -1) | (gz == CZ - 1), 0.0, 0.5 * time_step)
            z_edge = jnp.where((gz == 0) | (gz == CZ - 1), time_step, 0.0)
            even, odd = cond[z, 0:8], cond[z, 8:16]
            between = (0.5 * time_step) * (even + odd)
            beyond = x_inner * (odd + pltpu.roll(even, 7, 0))
            kx[z, 0:8] = between
            kx[z, 8:16] = beyond
            across = (between + pltpu.roll(beyond, 1, 0), between + beyond)
            for half in range(2):
                at = slice(8 * half, 8 * half + 8)
                c = (even, odd)[half]
                high = inner * (c + cond[z + 1, at])
                kz[z, at] = high
                side = y_inner * (c + pltpu.roll(c, 127, 1))
                ky[z, at] = side
                if flow[half] is not None:
                    total = across[half] + side + pltpu.roll(side, 1, 1) + high + flow[half]
                    total = total + c * (edges[half] + y_edge + z_edge)
                    diag = rate[z, at] + total
                    grow[0, z, at] = 1.0 + (1.0 - diag) * (1.0 / cheb_center)
                    for sweep, (a, b) in enumerate(pairs):
                        grow[sweep + 1, z, at] = (1.0 + a) - b * diag
                flow[half] = high


def operator_core_kernel(received, other, tables, *refs):
    def load(z, half):
        z = z - HALO
        return strided(received, 2 * ZB, z + ZB, half), strided(other, HALO + ZB, HALO + z, half)

    spans = [(range(HALO, HALO + ZB), range(HALO, HALO + ZB - 1), None)]
    operator_rows(refs, spans, load, tables)


def rim_rows(rim, back, part, other_part, upper, z, half):
    core = lax.axis_index("tm") & 1
    direct = strided(rim, HALO, 16 * HALO * part + z, half)
    handed = strided(back, HALO, 16 * HALO * other_part + z, half)
    return jnp.where(core == (0 if upper else 1), direct, handed)


def operator_rim_kernel(rim, back, tables, *refs):
    def load(z, half):
        upper = z < HALO
        z = z if upper else z - HALO - ZB
        return rim_rows(rim, back, 2, 2, upper, z, half), rim_rows(rim, back, 3, 1, upper, z, half)

    ends = HALO + ZB
    spans = [(range(0, HALO), range(0, HALO + 1), None), (range(ends, ZE), range(ends - 1, ZE - 1), ends - 2)]
    operator_rows(refs[8:], spans, load, tables)


def sweep_rows(buffers, operator, heated, j, spans):
    xa, xb, rhs = buffers
    kz, ky, kx, grow, heat, cavity = operator
    pairs = chebyshev()
    sweep = j % SWEEPS
    now, new = (xa, xb) if j % 2 == 0 else (xb, xa)
    halves = [slice(0, 8), slice(8, 16)]
    results = []
    for begin, end in spans:
        xs = {z: [now[z, at] for at in halves] for z in range(begin - 1, end + 1)}
        flows = {z: [kz[z, at] for at in halves] for z in range(begin - 1, end)}
        for z in range(begin, end):
            even, odd = xs[z]
            between, beyond = kx[z, 0:8], kx[z, 8:16]
            across = (
                between * odd + pltpu.roll(beyond * odd, 1, 0),
                between * even + beyond * pltpu.roll(even, 7, 0),
            )
            for half, at in enumerate(halves):
                v, side, keep = xs[z][half], ky[z, at], grow[sweep, z, at]
                total = flows[z][half] * xs[z + 1][half] + flows[z - 1][half] * xs[z - 1][half]
                total = across[half] + total
                total = total + (side * pltpu.roll(v, 127, 1) + pltpu.roll(side * v, 1, 1))
                if sweep == 0:
                    source = heat[z, at] + heated * cavity[z, at]
                    results.append((rhs, z, at, v + source))
                    value = keep * v + (total + source) * (1.0 / cheb_center)
                else:
                    a, b = pairs[sweep - 1]
                    value = (keep * v - a * new[z, at]) + b * (total + rhs[z, at])
                results.append((new, z, at, value))
    for ref, z, at, value in results:
        ref[z, at] = value


def melting(melt, j):
    return jnp.where(j // SWEEPS < melt[0], 1.0, 0.0)


def fine_core_kernel(melt, received, kz, ky, kx, grow, heat, cavity, xa, xb, rhs):
    for z in range(ZB):
        xa[HALO + z, 0:8] = strided(received, 2 * ZB, z, 0)
        xa[HALO + z, 8:16] = strided(received, 2 * ZB, z, 1)
    for j in range(EARLY):
        spans = [(HALO + j + 1, HALO + ZB - j - 1)]
        sweep_rows((xa, xb, rhs), (kz, ky, kx, grow, heat, cavity), melting(melt, j), j, spans)


def fine_kernel(melt, rim, back, kz, ky, kx, grow, heat, cavity, xa_in, xb_in, rhs_in, out, xa, xb, rhs):
    del xa_in, xb_in, rhs_in
    lane = lanes(8)
    for z in range(HALO):
        for half in range(2):
            at = slice(8 * half, 8 * half + 8)
            xa[z, at] = rim_rows(rim, back, 0, 0, True, z, half)
            xa[HALO + ZB + z, at] = rim_rows(rim, back, 0, 0, False, z, half)
    for j in range(HALO):
        spans = [(j + 1, ZE - 1 - j)]
        if j < EARLY:
            spans = [(j + 1, HALO + j + 1), (HALO + ZB - j - 1, ZE - 1 - j)]
        sweep_rows((xa, xb, rhs), (kz, ky, kx, grow, heat, cavity), melting(melt, j), j, spans)
    for z in range(ROWS):
        for half in range(2):
            at = slice(8 * half, 8 * half + 8)
            v = xa[HALO + z, at]
            if z < 24:
                side = pltpu.roll(xa[HALO + 40 + z % 8, at], 96 - 32 * (z // 8), 1)
            else:
                side = 0.0
            out[pl.ds(half * ROWS + z, 8, stride=2 * ROWS), :] = jnp.where(lane < YB, v, side)


def cycle_kernel(offsets, cells, base, out):
    b = lax.axis_index("tm")
    tiles = range(5)
    ids = [cells[b, 8 * i : 8 * i + 8] for i in tiles]
    lump = [base[b, 8 * i : 8 * i + 8] for i in tiles]
    fixed = [v > 0 for v in ids]
    spots = [jnp.where(fixed[i], ids[i] + (YB - 1), 0) for i in tiles]
    gain = [jnp.ones((8, 128), jnp.float32)] * 5
    shift = [jnp.zeros((8, 128), jnp.float32)] * 5
    gains = []
    for g in range(NT):
        table = offsets[g, 24:25, :]
        row = [
            1.0 / (lump[i] + jnp.where(fixed[i], lookup(table, spots[i]), 0.0)) for i in tiles
        ]
        gains.append(row)
        for i in tiles:
            gain[i] = row[i] * gain[i]
            shift[i] = row[i] * shift[i] + offsets[g, 8 * i : 8 * i + 8]
    value = [shift[i] / (1.0 - gain[i]) for i in tiles]
    for g in range(NT):
        for i in tiles:
            out[g, 8 * i : 8 * i + 8] = value[i]
            value[i] = gains[g][i] * value[i] + offsets[g, 8 * i : 8 * i + 8]


def unpack_kernel(folded, out):
    for by in range(2):
        parts = []
        for bz in range(8):
            parts = parts + unfold(folded[by * 8 + bz])
        whole = jnp.concatenate(parts, axis=0).T
        out[YB * by : YB * by + YB, :] = whole[0:YB]


VMEM = pl.BlockSpec(memory_space=pltpu.VMEM)
SMEM = pl.BlockSpec(memory_space=pltpu.SMEM)
HBM = pl.BlockSpec(memory_space=pl.ANY)


def call(kernel, outs, in_specs, scratch=(), limit=8, aliases={}, flops=0, nbytes=0):
    return pl.pallas_call(
        kernel,
        out_shape=outs,
        in_specs=in_specs,
        out_specs=jax.tree.map(lambda _: VMEM, outs),
        scratch_shapes=list(scratch),
        input_output_aliases=aliases,
        compiler_params=pltpu.CompilerParams(vmem_limit_bytes=limit * 1024 * 1024),
        cost_estimate=pl.CostEstimate(flops=flops, bytes_accessed=nbytes, transcendentals=0),
    )


def f32(*shape):
    return jax.ShapeDtypeStruct(shape, jnp.float32)


def i32(*shape):
    return jax.ShapeDtypeStruct(shape, jnp.int32)


def per_device(start_guess, material, channel, coolant_temp, htc_index, htc_levels, melt_steps):
    packed, rest, tables = call(
        pack_kernel,
        (f32(16, 2, ZB, 128), f32(16, ZB, 128), f32(8, 128)),
        [HBM] * 6,
        limit=LIMIT,
        scratch=[
            pltpu.VMEM((CY, CZ), jnp.float32),
            pltpu.VMEM((2, CY, CZ), jnp.int32),
            pltpu.VMEM((1, SEGS), jnp.float32),
            pltpu.VMEM((1, SEGS), jnp.int32),
            pltpu.SMEM((LEVELS,), jnp.float32),
            pltpu.SemaphoreType.DMA((6,)),
        ],
        nbytes=4000000,
    )(
        start_guess[0, 0],
        material[0],
        channel[0],
        coolant_temp,
        htc_index,
        htc_levels,
    )

    received = lax.all_to_all(packed, "space", 0, 0, tiled=True)

    swap = [(i, i ^ 1) for i in range(NT)]
    ahead = [
        (16 * tm + 8 * h + i + tm % 2, 16 * tm + 8 * h + i + 1 - tm % 2)
        for tm in range(NT)
        for h in range(2)
        for i in range(7)
    ]
    first_core = (lax.axis_index("tm") & 1) == 0
    field, label = received[:, 0], received[:, 1]
    top, bottom = slice(0, HALO), slice(HALO, ZB)
    away = jnp.where(first_core, field[:, top], field[:, bottom])
    other = lax.ppermute(jnp.concatenate([away, label], axis=1), "tm", swap)
    other_label = other[:, HALO:]
    sent = [
        jnp.where(first_core, field[:, bottom], field[:, top]),
        other[:, :HALO],
        jnp.where(first_core, label[:, bottom], label[:, top]),
        jnp.where(first_core, other_label[:, bottom], other_label[:, top]),
    ]
    rim = lax.ppermute(jnp.stack(sent), ("tm", "space"), ahead)

    flat = lambda v: v.reshape(-1, 128)
    plane = f32(ZE, 16, 128)
    planes = (plane,) * 5 + (f32(SWEEPS, ZE, 16, 128),) + (plane,) * 2
    received = flat(received)
    operator = call(operator_core_kernel, planes, [VMEM] * 3)(
        received, flat(other), tables
    )
    scaled, cells, base = call(
        coarse_kernel,
        (f32(16, ROWS, 128), i32(16, ROWS, 128), f32(16, ROWS, 128)),
        [VMEM] * 3,
        nbytes=2000000,
    )(packed, rest, tables)
    fields = call(
        fine_core_kernel, (plane,) * 3, [SMEM] + [VMEM] * 7
    )(melt_steps, received, *operator[2:])
    rim, first = lax.optimization_barrier((rim, fields[0]))
    fields = (first,) + tuple(fields[1:])
    back = flat(lax.ppermute(rim[1:4], "tm", swap))
    rim = flat(rim)
    operator = call(
        operator_rim_kernel,
        planes,
        [VMEM] * 11,
        aliases={3 + i: i for i in range(8)},
        flops=5000000,
        nbytes=4000000,
    )(rim, back, tables, *operator)
    fine, _, _, _ = call(
        fine_kernel,
        (f32(16 * ROWS, 128),) + (plane,) * 3,
        [SMEM] + [VMEM] * 11,
        aliases={9 + i: 1 + i for i in range(3)},
        flops=50000000,
        nbytes=4000000,
    )(melt_steps, rim, back, *operator[2:], *fields)
    fine = lax.all_to_all(fine.reshape(16, ROWS, 128), "space", 0, 0, tiled=True)

    offsets = lax.all_to_all(fine - scaled, "tm", 0, 0, tiled=True)
    starts = call(cycle_kernel, f32(16, ROWS, 128), [VMEM] * 3, nbytes=2000000)(
        offsets, cells, base
    )
    starts = lax.all_to_all(starts, "tm", 0, 0, tiled=True)
    unpack = call(unpack_kernel, f32(CY, CZ), [VMEM], nbytes=1000000)
    return unpack(starts)[None, None], unpack(fine)[None, None]


def solution(mesh):
    return jax.shard_map(
        per_device,
        mesh=mesh,
        in_specs=(
            P("tm", "space", None, None),
            P("space", None, None),
            P("space", None, None),
            P("tm", None),
            P("tm", None),
            P(),
            P("tm"),
        ),
        out_specs=(P("tm", "space", None, None), P("tm", "space", None, None)),
        check_vma=False,
    )
```

```python
import jax
import jax.numpy as jnp
from jax import lax
from jax.experimental import pallas as pl
from jax.experimental.pallas import tpu as pltpu
from jax.sharding import PartitionSpec as P

NT = 16
NX = 16
CY = 192
CZ = 384
STEPS = 4
SWEEPS = 6
SEGS = 32
LEVELS = 16

time_step = 0.25
melt_rate = 4.0
lam_high = 1.0 + time_step * (12.0 * 3.0 + 8.0)
cheb_center = 0.5 * (lam_high + 1.0)
cheb_half = 0.5 * (lam_high - 1.0)
cheb_ratio = cheb_center / cheb_half
lump_rate = 0.1 / NT

ZB = 48
HALO = STEPS * SWEEPS
ZE = ZB + 2 * HALO
YB = 96
PARTS = 16
SOLVED = ZB // PARTS * 16
EARLY = 23
LIMIT = 60


def chebyshev():
    rho = 1.0 / cheb_ratio
    pairs = []
    for _ in range(SWEEPS - 1):
        rho_next = 1.0 / (2.0 * cheb_ratio - rho)
        pairs.append((rho_next * rho, 2.0 * rho_next / cheb_half))
        rho = rho_next
    return pairs


def lanes(rows):
    return lax.broadcasted_iota(jnp.int32, (rows, 128), 1)


def lookup(row, index):
    return jnp.take_along_axis(jnp.broadcast_to(row, index.shape), index, axis=1, mode="promise_in_bounds")


def conductivity(material):
    return jnp.where(material == 0.0, 1.0, jnp.where(material == 1.0, 3.0, 0.6)).astype(jnp.float32)


def window(plane, by):
    part = plane[64 * by : 64 * by + 128, :].T
    return part if by == 0 else pltpu.roll(part, 96, 1)


def pack_kernel(
    start, material, channel, coolant, index, levels, packed, rest, tables, fields, labels, small, ids, steps, sems
):
    copies = [
        pltpu.make_async_copy(channel, labels.at[0], sems.at[0]),
        pltpu.make_async_copy(material, labels.at[1], sems.at[1]),
        pltpu.make_async_copy(start, fields, sems.at[2]),
        pltpu.make_async_copy(index, ids, sems.at[3]),
        pltpu.make_async_copy(coolant, small, sems.at[4]),
        pltpu.make_async_copy(levels, steps, sems.at[5]),
    ]
    for copy in copies:
        copy.start()
    core = lax.axis_index("tm") & 1
    tables[...] = jnp.zeros_like(tables)
    copies[0].wait()
    seg = [window(labels[0].astype(jnp.float32), by) for by in range(2)]
    copies[1].wait()
    mat = [window(labels[1].astype(jnp.float32), by) for by in range(2)]
    copies[2].wait()
    field = [window(fields[...], by) for by in range(2)]
    for by in range(2):
        mine = jnp.where(core == 0, mat[by], seg[by])
        theirs = jnp.where(core == 0, seg[by], mat[by])
        for bz in range(8):
            at = slice(ZB * bz, ZB * bz + ZB)
            packed[8 * by + bz, 0] = field[by][at]
            packed[8 * by + bz, 1] = mine[at]
            rest[8 * by + bz] = theirs[at]
    for copy in copies[3:]:
        copy.wait()
    tables[1:2, 0:SEGS] = small[...]
    tables[2:3, 0:SEGS] = ids[...].astype(jnp.float32)
    which = tables[2:3, :].astype(jnp.int32)
    picked = jnp.zeros((1, 128), jnp.float32)
    for level in range(LEVELS):
        picked = jnp.where(which == level, steps[level], picked)
    picked = jnp.where(lanes(1) < SEGS, picked, 0.0)
    heat = picked * tables[1:2, :]
    tables[0:1, :] = pltpu.roll(picked, 1, 1)
    tables[1:2, :] = pltpu.roll(heat, 1, 1)
    tables[2:3, :] = pltpu.roll(picked, YB, 1)


def coarse_kernel(packed, rest, tables, scaled, cells, base, all_cells, all_base):
    core = lax.axis_index("tm") & 1
    rate_table = tables[0:1, :]
    for b in range(16):
        for i in range(ZB // 8):
            at = slice(8 * i, 8 * i + 8)
            to = slice(ZB * b + 8 * i, ZB * b + 8 * i + 8)
            mine, theirs = packed[b, 1, at], rest[b, at]
            ids = jnp.where(core == 0, theirs, mine).astype(jnp.int32)
            lump = 1.0 + lump_rate * conductivity(jnp.where(core == 0, mine, theirs))
            scaled[to] = packed[b, 0, at] / (lump + lookup(rate_table, ids))
            all_cells[to] = ids
            all_base[to] = lump
    part = lax.axis_index("tm")
    for i in range(SOLVED // 8):
        rows = pl.ds(8 * PARTS * i + part, 8, stride=PARTS)
        cells[8 * i : 8 * i + 8] = all_cells[rows, :]
        base[8 * i : 8 * i + 8] = all_base[rows, :]


def strided(ref, pitch, at, half):
    return ref[pl.ds(half * pitch + at, 8, stride=2 * pitch), :]


def operator_rows(refs, spans, load, tables):
    cond, rate, kz, ky, kx, grow, heat, cavity = refs
    core = lax.axis_index("tm") & 1
    bz, by = lax.rem(lax.axis_index("space"), 8), lax.div(lax.axis_index("space"), 8)
    lane = lanes(8)
    sub = lax.broadcasted_iota(jnp.int32, (8, 128), 0)
    rate_table = tables[0:1, :]
    heat_table = tables[1:2, :]

    for fresh, _, _ in spans:
        for z in fresh:
            for half in range(2):
                to = slice(8 * half, 8 * half + 8)
                a, b = load(z, half)
                mat = jnp.where(core == 0, a, b)
                seg = jnp.where(core == 0, b, a).astype(jnp.int32)
                cond[z, to] = conductivity(mat)
                cavity[z, to] = jnp.where(mat == 2.0, time_step * melt_rate, 0.0)
                heat[z, to] = time_step * lookup(heat_table, seg)
                rate[z, to] = 1.0 + time_step * lookup(rate_table, seg)

    last = jnp.where(by == 0, 127, YB - 1)
    first = jnp.where(by == 0, 0, YB)
    y_inner = jnp.where(lane == last, 0.0, 0.5 * time_step)
    y_edge = jnp.where((lane == last) | (lane == first), time_step, 0.0)
    x_inner = jnp.where(sub == 7, 0.0, 0.5 * time_step)
    edges = (jnp.where(sub == 0, time_step, 0.0), jnp.where(sub == 7, time_step, 0.0))
    z0 = bz * ZB - HALO
    pairs = chebyshev()
    for _, faces, before in spans:
        flow = [None, None] if before is None else [kz[before, 0:8], kz[before, 8:16]]
        for z in faces:
            gz = z + z0
            inner = jnp.where((gz == -1) | (gz == CZ - 1), 0.0, 0.5 * time_step)
            z_edge = jnp.where((gz == 0) | (gz == CZ - 1), time_step, 0.0)
            even, odd = cond[z, 0:8], cond[z, 8:16]
            between = (0.5 * time_step) * (even + odd)
            beyond = x_inner * (odd + pltpu.roll(even, 7, 0))
            kx[z, 0:8] = between
            kx[z, 8:16] = beyond
            across = (between + pltpu.roll(beyond, 1, 0), between + beyond)
            for half in range(2):
                at = slice(8 * half, 8 * half + 8)
                c = (even, odd)[half]
                high = inner * (c + cond[z + 1, at])
                kz[z, at] = high
                side = y_inner * (c + pltpu.roll(c, 127, 1))
                ky[z, at] = side
                if flow[half] is not None:
                    total = across[half] + side + pltpu.roll(side, 1, 1) + high + flow[half]
                    total = total + c * (edges[half] + y_edge + z_edge)
                    diag = rate[z, at] + total
                    grow[0, z, at] = 1.0 + (1.0 - diag) * (1.0 / cheb_center)
                    for sweep, (a, b) in enumerate(pairs):
                        grow[sweep + 1, z, at] = (1.0 + a) - b * diag
                flow[half] = high


def operator_core_kernel(received, other, tables, *refs):
    refs, scaled = refs[:8], refs[8]

    def load(z, half):
        z = z - HALO
        return strided(received, 2 * ZB, z + ZB, half), strided(other, HALO + ZB, HALO + z, half)

    spans = [(range(HALO, HALO + ZB), range(HALO, HALO + ZB - 1), None)]
    operator_rows(refs, spans, load, tables)
    core = lax.axis_index("tm") & 1
    for z in range(ZB):
        for half in range(2):
            a, b = load(HALO + z, half)
            seg = jnp.where(core == 0, b, a).astype(jnp.int32)
            at = slice(8 * half, 8 * half + 8)
            lump = 1.0 + lump_rate * refs[0][HALO + z, at]
            scaled[z, at] = strided(received, 2 * ZB, z, half) / (lump + lookup(tables[0:1, :], seg))


def rim_rows(rim, back, part, other_part, upper, z, half):
    core = lax.axis_index("tm") & 1
    direct = strided(rim, HALO, 16 * HALO * part + z, half)
    handed = strided(back, HALO, 16 * HALO * other_part + z, half)
    return jnp.where(core == (0 if upper else 1), direct, handed)


def operator_rim_kernel(rim, back, tables, *refs):
    def load(z, half):
        upper = z < HALO
        z = z if upper else z - HALO - ZB
        return rim_rows(rim, back, 2, 2, upper, z, half), rim_rows(rim, back, 3, 1, upper, z, half)

    ends = HALO + ZB
    spans = [(range(0, HALO), range(0, HALO + 1), None), (range(ends, ZE), range(ends - 1, ZE - 1), ends - 2)]
    operator_rows(refs[8:], spans, load, tables)


def sweep_rows(buffers, operator, heated, j, spans):
    xa, xb, rhs = buffers
    kz, ky, kx, grow, heat, cavity = operator
    pairs = chebyshev()
    sweep = j % SWEEPS
    now, new = (xa, xb) if j % 2 == 0 else (xb, xa)
    halves = [slice(0, 8), slice(8, 16)]
    results = []
    for begin, end in spans:
        xs = {z: [now[z, at] for at in halves] for z in range(begin - 1, end + 1)}
        flows = {z: [kz[z, at] for at in halves] for z in range(begin - 1, end)}
        for z in range(begin, end):
            even, odd = xs[z]
            between, beyond = kx[z, 0:8], kx[z, 8:16]
            across = (
                between * odd + pltpu.roll(beyond * odd, 1, 0),
                between * even + beyond * pltpu.roll(even, 7, 0),
            )
            for half, at in enumerate(halves):
                v, side, keep = xs[z][half], ky[z, at], grow[sweep, z, at]
                total = flows[z][half] * xs[z + 1][half] + flows[z - 1][half] * xs[z - 1][half]
                total = across[half] + total
                total = total + (side * pltpu.roll(v, 127, 1) + pltpu.roll(side * v, 1, 1))
                if sweep == 0:
                    source = heat[z, at] + heated * cavity[z, at]
                    results.append((rhs, z, at, v + source))
                    value = keep * v + (total + source) * (1.0 / cheb_center)
                else:
                    a, b = pairs[sweep - 1]
                    value = (keep * v - a * new[z, at]) + b * (total + rhs[z, at])
                results.append((new, z, at, value))
    for ref, z, at, value in results:
        ref[z, at] = value


def melting(melt, j):
    return jnp.where(j // SWEEPS < melt[0], 1.0, 0.0)


def fine_core_kernel(melt, received, kz, ky, kx, grow, heat, cavity, xa, xb, rhs):
    for z in range(ZB):
        xa[HALO + z, 0:8] = strided(received, 2 * ZB, z, 0)
        xa[HALO + z, 8:16] = strided(received, 2 * ZB, z, 1)
    for j in range(EARLY):
        spans = [(HALO + j + 1, HALO + ZB - j - 1)]
        sweep_rows((xa, xb, rhs), (kz, ky, kx, grow, heat, cavity), melting(melt, j), j, spans)


def fine_kernel(
    melt, rim, back, scaled, tables, kz, ky, kx, grow, heat, cavity, xa_in, xb_in, rhs_in, out, xa, xb, rhs
):
    del xa_in, xb_in, rhs_in
    lane = lanes(8)
    for z in range(HALO):
        for half in range(2):
            at = slice(8 * half, 8 * half + 8)
            xa[z, at] = rim_rows(rim, back, 0, 0, True, z, half)
            xa[HALO + ZB + z, at] = rim_rows(rim, back, 0, 0, False, z, half)
    for j in range(HALO):
        spans = [(j + 1, ZE - 1 - j)]
        if j < EARLY:
            spans = [(j + 1, HALO + j + 1), (HALO + ZB - j - 1, ZE - 1 - j)]
        sweep_rows((xa, xb, rhs), (kz, ky, kx, grow, heat, cavity), melting(melt, j), j, spans)
    rates = tables[2:3, :]
    for z in range(ZB):
        for half in range(2):
            at = slice(8 * half, 8 * half + 8)
            value = xa[HALO + z, at] - scaled[z, at]
            first = 3 * (16 * (z % PARTS) + half) + z // PARTS
            out[pl.ds(first, 8, stride=6), :] = jnp.where(lane < YB, value, rates)


def cycle_kernel(offsets, cells, base, out):
    count = SOLVED // 8
    tiles = range(count)
    lane = lanes(8)
    ids = [cells[8 * i : 8 * i + 8] for i in tiles]
    lump = [base[8 * i : 8 * i + 8] for i in tiles]
    fixed = [v > 0 for v in ids]
    spots = [jnp.where(fixed[i], ids[i] + (YB - 1), 0) for i in tiles]
    gain = [jnp.ones((8, 128), jnp.float32)] * count
    shift = [jnp.zeros((8, 128), jnp.float32)] * count
    gains = []

    def given(g, i):
        return offsets[SOLVED * g + 8 * i : SOLVED * g + 8 * i + 8]

    for g in range(NT):
        table = offsets[SOLVED * g : SOLVED * g + 1, :]
        row = [
            1.0 / (lump[i] + jnp.where(fixed[i], lookup(table, spots[i]), 0.0)) for i in tiles
        ]
        gains.append(row)
        for i in tiles:
            gain[i] = row[i] * gain[i]
            shift[i] = row[i] * shift[i] + given(g, i)
    value = [shift[i] / (1.0 - gain[i]) for i in tiles]
    for g in range(NT):
        for i in tiles:
            side = pltpu.roll(given(g, 3 + i % 3), 96 if i < 3 else 64, 1)
            out[g, 8 * i : 8 * i + 8] = jnp.where(lane < YB, value[i], side)
        for i in range(3):
            side = pltpu.roll(given(g, 3 + i), 32, 1)
            out[g, SOLVED + 8 * i : SOLVED + 8 * i + 8] = jnp.where(lane < YB, given(g, i), side)
        for i in tiles:
            value[i] = gains[g][i] * value[i] + given(g, i)


def unpack_kernel(folded, scaled, starts, ends, new, fine):
    lane = lanes(8)
    for part in range(PARTS):
        for i in range(SOLVED // 8):
            rows = pl.ds(8 * PARTS * i + part, 8, stride=PARTS)
            new[rows, :] = folded[part, 8 * i : 8 * i + 8]
            if i < 3:
                fine[rows, :] = folded[part, SOLVED + 8 * i : SOLVED + 8 * i + 8]
            else:
                side = [folded[part, 24 * k + 8 * (i - 3) : 24 * k + 8 * (i - 3) + 8] for k in range(3)]
                side = [pltpu.roll(side[k], 32 + 32 * k, 1) for k in range(3)]
                fine[rows, :] = jnp.where(lane < 32, side[0], jnp.where(lane < 64, side[1], side[2]))
    for by in range(2):
        at, to = slice(CZ * by, CZ * by + CZ), slice(YB * by, YB * by + YB)
        starts[to, :] = new[at].T[0:YB]
        ends[to, :] = (fine[at] + scaled[at]).T[0:YB]


VMEM = pl.BlockSpec(memory_space=pltpu.VMEM)
SMEM = pl.BlockSpec(memory_space=pltpu.SMEM)
HBM = pl.BlockSpec(memory_space=pl.ANY)


def call(kernel, outs, in_specs, scratch=(), limit=8, aliases={}, flops=0, nbytes=0):
    return pl.pallas_call(
        kernel,
        out_shape=outs,
        in_specs=in_specs,
        out_specs=jax.tree.map(lambda _: VMEM, outs),
        scratch_shapes=list(scratch),
        input_output_aliases=aliases,
        compiler_params=pltpu.CompilerParams(vmem_limit_bytes=limit * 1024 * 1024),
        cost_estimate=pl.CostEstimate(flops=flops, bytes_accessed=nbytes, transcendentals=0),
    )


def f32(*shape):
    return jax.ShapeDtypeStruct(shape, jnp.float32)


def i32(*shape):
    return jax.ShapeDtypeStruct(shape, jnp.int32)


def per_device(start_guess, material, channel, coolant_temp, htc_index, htc_levels, melt_steps):
    packed, rest, tables = call(
        pack_kernel,
        (f32(16, 2, ZB, 128), f32(16, ZB, 128), f32(8, 128)),
        [HBM] * 6,
        limit=LIMIT,
        scratch=[
            pltpu.VMEM((CY, CZ), jnp.float32),
            pltpu.VMEM((2, CY, CZ), jnp.int32),
            pltpu.VMEM((1, SEGS), jnp.float32),
            pltpu.VMEM((1, SEGS), jnp.int32),
            pltpu.SMEM((LEVELS,), jnp.float32),
            pltpu.SemaphoreType.DMA((6,)),
        ],
        nbytes=4000000,
    )(
        start_guess[0, 0],
        material[0],
        channel[0],
        coolant_temp,
        htc_index,
        htc_levels,
    )

    received = lax.all_to_all(packed, "space", 0, 0, tiled=True)

    swap = [(i, i ^ 1) for i in range(NT)]
    ahead = [
        (16 * tm + 8 * h + i + tm % 2, 16 * tm + 8 * h + i + 1 - tm % 2)
        for tm in range(NT)
        for h in range(2)
        for i in range(7)
    ]
    first_core = (lax.axis_index("tm") & 1) == 0
    field, label = received[:, 0], received[:, 1]
    top, bottom = slice(0, HALO), slice(HALO, ZB)
    away = jnp.where(first_core, field[:, top], field[:, bottom])
    other = lax.ppermute(jnp.concatenate([away, label], axis=1), "tm", swap)
    other_label = other[:, HALO:]
    sent = [
        jnp.where(first_core, field[:, bottom], field[:, top]),
        other[:, :HALO],
        jnp.where(first_core, label[:, bottom], label[:, top]),
        jnp.where(first_core, other_label[:, bottom], other_label[:, top]),
    ]
    rim = lax.ppermute(jnp.stack(sent), ("tm", "space"), ahead)

    flat = lambda v: v.reshape(-1, 128)
    plane = f32(ZE, 16, 128)
    planes = (plane,) * 5 + (f32(SWEEPS, ZE, 16, 128),) + (plane,) * 2
    received = flat(received)
    *operator, own_scaled = call(operator_core_kernel, planes + (f32(ZB, 16, 128),), [VMEM] * 3)(
        received, flat(other), tables
    )
    scaled, cells, base = call(
        coarse_kernel,
        (f32(16 * ZB, 128), i32(SOLVED, 128), f32(SOLVED, 128)),
        [VMEM] * 3,
        scratch=[pltpu.VMEM((16 * ZB, 128), jnp.int32), pltpu.VMEM((16 * ZB, 128), jnp.float32)],
        nbytes=2000000,
    )(packed, rest, tables)
    fields = call(
        fine_core_kernel, (plane,) * 3, [SMEM] + [VMEM] * 7
    )(melt_steps, received, *operator[2:])
    rim, first = lax.optimization_barrier((rim, fields[0]))
    fields = (first,) + tuple(fields[1:])
    back = flat(lax.ppermute(rim[1:4], "tm", swap))
    rim = flat(rim)
    operator = call(
        operator_rim_kernel,
        planes,
        [VMEM] * 11,
        aliases={3 + i: i for i in range(8)},
        flops=5000000,
        nbytes=4000000,
    )(rim, back, tables, *operator)
    offsets, _, _, _ = call(
        fine_kernel,
        (f32(256 * 3, 128),) + (plane,) * 3,
        [SMEM] + [VMEM] * 13,
        aliases={11 + i: 1 + i for i in range(3)},
        flops=50000000,
        nbytes=4000000,
    )(melt_steps, rim, back, own_scaled, tables, *operator[2:], *fields)

    offsets = lax.all_to_all(offsets.reshape(256, 1, 384), ("tm", "space"), 0, 0, tiled=True)
    both = call(cycle_kernel, f32(NT, 72, 128), [VMEM] * 3, nbytes=2000000)(
        flat(offsets), cells, base
    )
    both = lax.all_to_all(both, "tm", 0, 0, tiled=True)
    starts, ends = call(
        unpack_kernel,
        (f32(CY, CZ), f32(CY, CZ)),
        [VMEM] * 2,
        scratch=[pltpu.VMEM((16 * ZB, 128), jnp.float32)] * 2,
        nbytes=2000000,
    )(both, scaled)
    return starts[None, None], ends[None, None]


def solution(mesh):
    return jax.shard_map(
        per_device,
        mesh=mesh,
        in_specs=(
            P("tm", "space", None, None),
            P("space", None, None),
            P("space", None, None),
            P("tm", None),
            P("tm", None),
            P(),
            P("tm"),
        ),
        out_specs=(P("tm", "space", None, None), P("tm", "space", None, None)),
        check_vma=False,
    )
```

```python
import jax
import jax.numpy as jnp
from jax import lax
from jax.experimental import pallas as pl
from jax.experimental.pallas import tpu as pltpu
from jax.sharding import PartitionSpec as P

NT = 16
NX = 16
CY = 192
CZ = 384
STEPS = 4
SWEEPS = 6
SEGS = 32
LEVELS = 16

time_step = 0.25
melt_rate = 4.0
lam_high = 1.0 + time_step * (12.0 * 3.0 + 8.0)
cheb_center = 0.5 * (lam_high + 1.0)
cheb_half = 0.5 * (lam_high - 1.0)
cheb_ratio = cheb_center / cheb_half
lump_rate = 0.1 / NT

ZB = 48
HALO = STEPS * SWEEPS
ZE = ZB + 2 * HALO
YB = 96
PARTS = 16
SOLVED = ZB // PARTS * 16
EARLY = 23
LIMIT = 60


def chebyshev():
    rho = 1.0 / cheb_ratio
    pairs = []
    for _ in range(SWEEPS - 1):
        rho_next = 1.0 / (2.0 * cheb_ratio - rho)
        pairs.append((rho_next * rho, 2.0 * rho_next / cheb_half))
        rho = rho_next
    return pairs


def lanes(rows):
    return lax.broadcasted_iota(jnp.int32, (rows, 128), 1)


def lookup(row, index):
    return jnp.take_along_axis(jnp.broadcast_to(row, index.shape), index, axis=1, mode="promise_in_bounds")


def conductivity(material):
    return jnp.where(material == 0.0, 1.0, jnp.where(material == 1.0, 3.0, 0.6)).astype(jnp.float32)


def window(plane, by):
    part = plane[64 * by : 64 * by + 128, :].T
    return part if by == 0 else pltpu.roll(part, 96, 1)


def pack_kernel(
    start, material, channel, coolant, index, levels, packed, rest, tables, fields, labels, small, ids, steps, sems
):
    copies = [
        pltpu.make_async_copy(channel, labels.at[0], sems.at[0]),
        pltpu.make_async_copy(material, labels.at[1], sems.at[1]),
        pltpu.make_async_copy(start, fields, sems.at[2]),
        pltpu.make_async_copy(index, ids, sems.at[3]),
        pltpu.make_async_copy(coolant, small, sems.at[4]),
        pltpu.make_async_copy(levels, steps, sems.at[5]),
    ]
    for copy in copies:
        copy.start()
    core = lax.axis_index("tm") & 1
    tables[...] = jnp.zeros_like(tables)
    copies[0].wait()
    seg = [window(labels[0].astype(jnp.float32), by) for by in range(2)]
    copies[1].wait()
    mat = [window(labels[1].astype(jnp.float32), by) for by in range(2)]
    copies[2].wait()
    field = [window(fields[...], by) for by in range(2)]
    for by in range(2):
        mine = jnp.where(core == 0, mat[by], seg[by])
        theirs = jnp.where(core == 0, seg[by], mat[by])
        for bz in range(8):
            at = slice(ZB * bz, ZB * bz + ZB)
            packed[8 * by + bz, 0] = field[by][at]
            packed[8 * by + bz, 1] = mine[at]
            rest[8 * by + bz] = theirs[at]
    for copy in copies[3:]:
        copy.wait()
    tables[1:2, 0:SEGS] = small[...]
    tables[2:3, 0:SEGS] = ids[...].astype(jnp.float32)
    which = tables[2:3, :].astype(jnp.int32)
    picked = jnp.zeros((1, 128), jnp.float32)
    for level in range(LEVELS):
        picked = jnp.where(which == level, steps[level], picked)
    picked = jnp.where(lanes(1) < SEGS, picked, 0.0)
    heat = picked * tables[1:2, :]
    tables[0:1, :] = pltpu.roll(picked, 1, 1)
    tables[1:2, :] = pltpu.roll(heat, 1, 1)
    tables[2:3, :] = pltpu.roll(picked, YB, 1)


def coarse_kernel(packed, rest, tables, scaled, cells, base, all_cells, all_base):
    core = lax.axis_index("tm") & 1
    rate_table = tables[0:1, :]
    for b in range(16):
        for i in range(ZB // 8):
            at = slice(8 * i, 8 * i + 8)
            to = slice(ZB * b + 8 * i, ZB * b + 8 * i + 8)
            mine, theirs = packed[b, 1, at], rest[b, at]
            ids = jnp.where(core == 0, theirs, mine).astype(jnp.int32)
            lump = 1.0 + lump_rate * conductivity(jnp.where(core == 0, mine, theirs))
            scaled[to] = packed[b, 0, at] / (lump + lookup(rate_table, ids))
            all_cells[to] = ids
            all_base[to] = lump
    part = lax.axis_index("tm")
    for i in range(SOLVED // 8):
        rows = pl.ds(8 * PARTS * i + part, 8, stride=PARTS)
        cells[8 * i : 8 * i + 8] = all_cells[rows, :]
        base[8 * i : 8 * i + 8] = all_base[rows, :]


def strided(ref, pitch, at, half):
    return ref[pl.ds(half * pitch + at, 8, stride=2 * pitch), :]


def turned(i, count):
    return i + (lax.axis_index("tm") & 1) * (count - 1 - 2 * i)


def operator_rows(refs, spans, load, tables):
    cond, rate, kz, ky, kx, grow, heat, cavity = refs
    core = lax.axis_index("tm") & 1
    bz, by = lax.rem(lax.axis_index("space"), 8), lax.div(lax.axis_index("space"), 8)
    lane = lanes(8)
    sub = lax.broadcasted_iota(jnp.int32, (8, 128), 0)
    rate_table = tables[0:1, :]
    heat_table = tables[1:2, :]

    for fresh, _, _ in spans:
        for z in fresh:
            for half in range(2):
                to = slice(8 * half, 8 * half + 8)
                a, b = load(z, half)
                mat = jnp.where(core == 0, a, b)
                seg = jnp.where(core == 0, b, a).astype(jnp.int32)
                cond[z, to] = conductivity(mat)
                cavity[z, to] = jnp.where(mat == 2.0, time_step * melt_rate, 0.0)
                heat[z, to] = time_step * lookup(heat_table, seg)
                rate[z, to] = 1.0 + time_step * lookup(rate_table, seg)

    last = jnp.where(by == 0, 127, YB - 1)
    first = jnp.where(by == 0, 0, YB)
    y_inner = jnp.where(lane == last, 0.0, 0.5 * time_step)
    y_edge = jnp.where((lane == last) | (lane == first), time_step, 0.0)
    x_inner = jnp.where(sub == 7, 0.0, 0.5 * time_step)
    edges = (jnp.where(sub == 0, time_step, 0.0), jnp.where(sub == 7, time_step, 0.0))
    z0 = bz * ZB - HALO
    pairs = chebyshev()
    for _, faces, before in spans:
        flow = [None, None] if before is None else [kz[before, 0:8], kz[before, 8:16]]
        for z in faces:
            gz = z0 + turned(z, ZE)
            between_z = gz - core
            inner = jnp.where((between_z == -1) | (between_z == CZ - 1), 0.0, 0.5 * time_step)
            z_edge = jnp.where((gz == 0) | (gz == CZ - 1), time_step, 0.0)
            even, odd = cond[z, 0:8], cond[z, 8:16]
            between = (0.5 * time_step) * (even + odd)
            beyond = x_inner * (odd + pltpu.roll(even, 7, 0))
            kx[z, 0:8] = between
            kx[z, 8:16] = beyond
            across = (between + pltpu.roll(beyond, 1, 0), between + beyond)
            for half in range(2):
                at = slice(8 * half, 8 * half + 8)
                c = (even, odd)[half]
                high = inner * (c + cond[z + 1, at])
                kz[z, at] = high
                side = y_inner * (c + pltpu.roll(c, 127, 1))
                ky[z, at] = side
                if flow[half] is not None:
                    total = across[half] + side + pltpu.roll(side, 1, 1) + high + flow[half]
                    total = total + c * (edges[half] + y_edge + z_edge)
                    diag = rate[z, at] + total
                    grow[0, z, at] = 1.0 + (1.0 - diag) * (1.0 / cheb_center)
                    for sweep, (a, b) in enumerate(pairs):
                        grow[sweep + 1, z, at] = (1.0 + a) - b * diag
                flow[half] = high


def operator_core_kernel(received, other, tables, *refs):
    refs, scaled = refs[:8], refs[8]

    def load(z, half):
        z = turned(z - HALO, ZB)
        return strided(received, 2 * ZB, z + ZB, half), strided(other, HALO + ZB, HALO + z, half)

    spans = [(range(HALO, HALO + ZB), range(HALO, HALO + ZB - 1), None)]
    operator_rows(refs, spans, load, tables)
    core = lax.axis_index("tm") & 1
    for z in range(ZB):
        for half in range(2):
            a, b = load(HALO + z, half)
            seg = jnp.where(core == 0, b, a).astype(jnp.int32)
            at = slice(8 * half, 8 * half + 8)
            lump = 1.0 + lump_rate * refs[0][HALO + z, at]
            scaled[z, at] = strided(received, 2 * ZB, turned(z, ZB), half) / (lump + lookup(tables[0:1, :], seg))


def sweep_rows(buffers, operator, heated, j, spans):
    xa, xb, rhs = buffers
    kz, ky, kx, grow, heat, cavity = operator
    pairs = chebyshev()
    sweep = j % SWEEPS
    now, new = (xa, xb) if j % 2 == 0 else (xb, xa)
    halves = [slice(0, 8), slice(8, 16)]
    results = []
    for begin, end in spans:
        xs = {z: [now[z, at] for at in halves] for z in range(begin - 1, end + 1)}
        flows = {z: [kz[z, at] for at in halves] for z in range(begin - 1, end)}
        for z in range(begin, end):
            even, odd = xs[z]
            between, beyond = kx[z, 0:8], kx[z, 8:16]
            across = (
                between * odd + pltpu.roll(beyond * odd, 1, 0),
                between * even + beyond * pltpu.roll(even, 7, 0),
            )
            for half, at in enumerate(halves):
                v, side, keep = xs[z][half], ky[z, at], grow[sweep, z, at]
                total = flows[z][half] * xs[z + 1][half] + flows[z - 1][half] * xs[z - 1][half]
                total = across[half] + total
                total = total + (side * pltpu.roll(v, 127, 1) + pltpu.roll(side * v, 1, 1))
                if sweep == 0:
                    source = heat[z, at] + heated * cavity[z, at]
                    results.append((rhs, z, at, v + source))
                    value = keep * v + (total + source) * (1.0 / cheb_center)
                else:
                    a, b = pairs[sweep - 1]
                    value = (keep * v - a * new[z, at]) + b * (total + rhs[z, at])
                results.append((new, z, at, value))
    for ref, z, at, value in results:
        ref[z, at] = value


def melting(melt, j):
    return jnp.where(j // SWEEPS < melt[0], 1.0, 0.0)


def fine_core_kernel(melt, received, kz, ky, kx, grow, heat, cavity, xa, xb, rhs):
    for z in range(ZB):
        row = turned(z, ZB)
        xa[HALO + z, 0:8] = strided(received, 2 * ZB, row, 0)
        xa[HALO + z, 8:16] = strided(received, 2 * ZB, row, 1)
    for j in range(EARLY):
        spans = [(HALO + j + 1, HALO + ZB - j - 1)]
        sweep_rows((xa, xb, rhs), (kz, ky, kx, grow, heat, cavity), melting(melt, j), j, spans)


def rim_sweeps(melt, halo, tables, refs, spans, mine, other):
    operator, buffers = refs[:8], refs[8:]
    start = spans[0][0][0]

    def load(part, z, half):
        return strided(halo, HALO, 16 * HALO * part + turned(z - start, HALO), half)

    operator_rows(operator, spans, lambda z, half: (load(mine, z, half), load(other, z, half)), tables)
    for z in spans[0][0]:
        buffers[0][z, 0:8] = load(0, z, 0)
        buffers[0][z, 8:16] = load(0, z, 1)
    for j in range(EARLY):
        rows = (j + 1, HALO + j + 1) if start == 0 else (HALO + ZB - j - 1, ZE - 1 - j)
        sweep_rows(buffers, operator[2:], melting(melt, j), j, [rows])


def fine_upper_kernel(melt, rim, tables, *refs):
    rim_sweeps(melt, rim, tables, refs[11:], [(range(0, HALO), range(0, HALO + 1), None)], 2, 3)


def fine_lower_kernel(melt, back, scaled, tables, *refs):
    out, refs = refs[11], refs[12:]
    ends = HALO + ZB
    rim_sweeps(melt, back, tables, refs, [(range(ends, ZE), range(ends - 1, ZE - 1), ends - 2)], 2, 1)
    buffers, j = refs[8:], HALO - 1
    sweep_rows(buffers, refs[2:8], melting(melt, j), j, [(HALO, HALO + ZB)])
    lane = lanes(8)
    rates = tables[2:3, :]
    for z in range(ZB):
        row = turned(z, ZB)
        for half in range(2):
            at = slice(8 * half, 8 * half + 8)
            value = buffers[0][HALO + z, at] - scaled[z, at]
            first = 3 * (16 * (row & (PARTS - 1)) + half) + (row >> 4)
            out[pl.ds(first, 8, stride=6), :] = jnp.where(lane < YB, value, rates)


def cycle_kernel(offsets, cells, base, out):
    count = SOLVED // 8
    tiles = range(count)
    lane = lanes(8)
    ids = [cells[8 * i : 8 * i + 8] for i in tiles]
    lump = [base[8 * i : 8 * i + 8] for i in tiles]
    fixed = [v > 0 for v in ids]
    spots = [jnp.where(fixed[i], ids[i] + (YB - 1), 0) for i in tiles]
    gain = [jnp.ones((8, 128), jnp.float32)] * count
    shift = [jnp.zeros((8, 128), jnp.float32)] * count
    gains = []

    def given(g, i):
        return offsets[SOLVED * g + 8 * i : SOLVED * g + 8 * i + 8]

    for g in range(NT):
        table = offsets[SOLVED * g : SOLVED * g + 1, :]
        row = [
            1.0 / (lump[i] + jnp.where(fixed[i], lookup(table, spots[i]), 0.0)) for i in tiles
        ]
        gains.append(row)
        for i in tiles:
            gain[i] = row[i] * gain[i]
            shift[i] = row[i] * shift[i] + given(g, i)
    value = [shift[i] / (1.0 - gain[i]) for i in tiles]
    for g in range(NT):
        for i in tiles:
            side = pltpu.roll(given(g, 3 + i % 3), 96 if i < 3 else 64, 1)
            out[g, 8 * i : 8 * i + 8] = jnp.where(lane < YB, value[i], side)
        for i in range(3):
            side = pltpu.roll(given(g, 3 + i), 32, 1)
            out[g, SOLVED + 8 * i : SOLVED + 8 * i + 8] = jnp.where(lane < YB, given(g, i), side)
        for i in tiles:
            value[i] = gains[g][i] * value[i] + given(g, i)


def unpack_kernel(folded, scaled, starts, ends, new, fine):
    lane = lanes(8)
    for part in range(PARTS):
        for i in range(SOLVED // 8):
            rows = pl.ds(8 * PARTS * i + part, 8, stride=PARTS)
            new[rows, :] = folded[part, 8 * i : 8 * i + 8]
            if i < 3:
                fine[rows, :] = folded[part, SOLVED + 8 * i : SOLVED + 8 * i + 8]
            else:
                side = [folded[part, 24 * k + 8 * (i - 3) : 24 * k + 8 * (i - 3) + 8] for k in range(3)]
                side = [pltpu.roll(side[k], 32 + 32 * k, 1) for k in range(3)]
                fine[rows, :] = jnp.where(lane < 32, side[0], jnp.where(lane < 64, side[1], side[2]))
    for by in range(2):
        at, to = slice(CZ * by, CZ * by + CZ), slice(YB * by, YB * by + YB)
        starts[to, :] = new[at].T[0:YB]
        ends[to, :] = (fine[at] + scaled[at]).T[0:YB]


VMEM = pl.BlockSpec(memory_space=pltpu.VMEM)
SMEM = pl.BlockSpec(memory_space=pltpu.SMEM)
HBM = pl.BlockSpec(memory_space=pl.ANY)


def call(kernel, outs, in_specs, scratch=(), limit=8, aliases={}, flops=0, nbytes=0):
    return pl.pallas_call(
        kernel,
        out_shape=outs,
        in_specs=in_specs,
        out_specs=jax.tree.map(lambda _: VMEM, outs),
        scratch_shapes=list(scratch),
        input_output_aliases=aliases,
        compiler_params=pltpu.CompilerParams(vmem_limit_bytes=limit * 1024 * 1024),
        cost_estimate=pl.CostEstimate(flops=flops, bytes_accessed=nbytes, transcendentals=0),
    )


def f32(*shape):
    return jax.ShapeDtypeStruct(shape, jnp.float32)


def i32(*shape):
    return jax.ShapeDtypeStruct(shape, jnp.int32)


def per_device(start_guess, material, channel, coolant_temp, htc_index, htc_levels, melt_steps):
    packed, rest, tables = call(
        pack_kernel,
        (f32(16, 2, ZB, 128), f32(16, ZB, 128), f32(8, 128)),
        [HBM] * 6,
        limit=LIMIT,
        scratch=[
            pltpu.VMEM((CY, CZ), jnp.float32),
            pltpu.VMEM((2, CY, CZ), jnp.int32),
            pltpu.VMEM((1, SEGS), jnp.float32),
            pltpu.VMEM((1, SEGS), jnp.int32),
            pltpu.SMEM((LEVELS,), jnp.float32),
            pltpu.SemaphoreType.DMA((6,)),
        ],
        nbytes=4000000,
    )(
        start_guess[0, 0],
        material[0],
        channel[0],
        coolant_temp,
        htc_index,
        htc_levels,
    )

    received = lax.all_to_all(packed, "space", 0, 0, tiled=True)

    swap = [(i, i ^ 1) for i in range(NT)]
    ahead = [
        (16 * tm + 8 * h + i + tm % 2, 16 * tm + 8 * h + i + 1 - tm % 2)
        for tm in range(NT)
        for h in range(2)
        for i in range(7)
    ]
    first_core = (lax.axis_index("tm") & 1) == 0
    field, label = received[:, 0], received[:, 1]
    top, bottom = slice(0, HALO), slice(HALO, ZB)
    away = jnp.where(first_core, field[:, top], field[:, bottom])
    other = lax.ppermute(jnp.concatenate([away, label], axis=1), "tm", swap)
    other_label = other[:, HALO:]
    sent = [
        jnp.where(first_core, field[:, bottom], field[:, top]),
        other[:, :HALO],
        jnp.where(first_core, label[:, bottom], label[:, top]),
        jnp.where(first_core, other_label[:, bottom], other_label[:, top]),
    ]
    rim = lax.ppermute(jnp.stack(sent), ("tm", "space"), ahead)

    flat = lambda v: v.reshape(-1, 128)
    plane = f32(ZE, 16, 128)
    planes = (plane,) * 5 + (f32(SWEEPS, ZE, 16, 128),) + (plane,) * 2
    received = flat(received)
    *operator, own_scaled = call(operator_core_kernel, planes + (f32(ZB, 16, 128),), [VMEM] * 3)(
        received, flat(other), tables
    )
    scaled, cells, base = call(
        coarse_kernel,
        (f32(16 * ZB, 128), i32(SOLVED, 128), f32(SOLVED, 128)),
        [VMEM] * 3,
        scratch=[pltpu.VMEM((16 * ZB, 128), jnp.int32), pltpu.VMEM((16 * ZB, 128), jnp.float32)],
        nbytes=2000000,
    )(packed, rest, tables)
    fields = call(
        fine_core_kernel, (plane,) * 3, [SMEM] + [VMEM] * 7
    )(melt_steps, received, *operator[2:])
    rim, first, scaled = lax.optimization_barrier((rim, fields[0], scaled))
    fields = (first,) + tuple(fields[1:])
    back = flat(lax.ppermute(rim[1:4], "tm", swap))
    rim = flat(rim)
    state = call(
        fine_upper_kernel,
        planes + (plane,) * 3,
        [SMEM] + [VMEM] * 13,
        aliases={3 + i: i for i in range(11)},
        flops=20000000,
        nbytes=4000000,
    )(melt_steps, rim, tables, *operator, *fields)
    offsets = call(
        fine_lower_kernel,
        (f32(256 * 3, 128),) + planes + (plane,) * 3,
        [SMEM] + [VMEM] * 14,
        aliases={4 + i: 1 + i for i in range(11)},
        flops=20000000,
        nbytes=4000000,
    )(melt_steps, back, own_scaled, tables, *state)[0]

    offsets = lax.all_to_all(offsets.reshape(256, 1, 384), ("tm", "space"), 0, 0, tiled=True)
    both = call(cycle_kernel, f32(NT, 72, 128), [VMEM] * 3, nbytes=2000000)(
        flat(offsets), cells, base
    )
    both = lax.all_to_all(both, "tm", 0, 0, tiled=True)
    starts, ends = call(
        unpack_kernel,
        (f32(CY, CZ), f32(CY, CZ)),
        [VMEM] * 2,
        scratch=[pltpu.VMEM((16 * ZB, 128), jnp.float32)] * 2,
        nbytes=2000000,
    )(both, scaled)
    return starts[None, None], ends[None, None]


def solution(mesh):
    return jax.shard_map(
        per_device,
        mesh=mesh,
        in_specs=(
            P("tm", "space", None, None),
            P("space", None, None),
            P("space", None, None),
            P("tm", None),
            P("tm", None),
            P(),
            P("tm"),
        ),
        out_specs=(P("tm", "space", None, None), P("tm", "space", None, None)),
        check_vma=False,
    )
```

```python
import jax
import jax.numpy as jnp
from jax import lax
from jax.experimental import pallas as pl
from jax.experimental.pallas import tpu as pltpu
from jax.sharding import PartitionSpec as P

NT = 16
NX = 16
CY = 192
CZ = 384
STEPS = 4
SWEEPS = 6
SEGS = 32
LEVELS = 16

time_step = 0.25
melt_rate = 4.0
lam_high = 1.0 + time_step * (12.0 * 3.0 + 8.0)
cheb_center = 0.5 * (lam_high + 1.0)
cheb_half = 0.5 * (lam_high - 1.0)
cheb_ratio = cheb_center / cheb_half
lump_rate = 0.1 / NT

ZB = 48
HALO = STEPS * SWEEPS
ZE = ZB + 2 * HALO
YB = 96
PARTS = 16
SOLVED = ZB // PARTS * 16
EARLY = 23
LIMIT = 60


def chebyshev():
    rho = 1.0 / cheb_ratio
    pairs = []
    for _ in range(SWEEPS - 1):
        rho_next = 1.0 / (2.0 * cheb_ratio - rho)
        pairs.append((rho_next * rho, 2.0 * rho_next / cheb_half))
        rho = rho_next
    return pairs


def lanes(rows):
    return lax.broadcasted_iota(jnp.int32, (rows, 128), 1)


def lookup(row, index):
    return jnp.take_along_axis(jnp.broadcast_to(row, index.shape), index, axis=1, mode="promise_in_bounds")


def conductivity(material):
    return jnp.where(material == 0.0, 1.0, jnp.where(material == 1.0, 3.0, 0.6)).astype(jnp.float32)


def window(plane, by):
    part = plane[64 * by : 64 * by + 128, :].T
    return part if by == 0 else pltpu.roll(part, 96, 1)


def pack_kernel(start, material, channel, packed, fields, labels, blocks, sems):
    copies = [
        pltpu.make_async_copy(channel, labels.at[0], sems.at[0]),
        pltpu.make_async_copy(material, labels.at[1], sems.at[1]),
        pltpu.make_async_copy(start, fields, sems.at[2]),
    ]
    for copy in copies:
        copy.start()
    core = lax.axis_index("tm") & 1
    copies[0].wait()
    copies[1].wait()
    label = jnp.where(core == 0, labels[1], labels[0]).astype(jnp.float32)
    for by in range(2):
        mine = window(label, by)
        for bz in range(8):
            blocks[8 * by + bz, 1] = mine[ZB * bz : ZB * bz + ZB]
    copies[2].wait()
    sent = []
    for by in range(2):
        field = window(fields[...], by)
        for bz in range(8):
            blocks[8 * by + bz, 0] = field[ZB * bz : ZB * bz + ZB]
        half = pl.ds(8 * by, 8)
        sent.append(pltpu.make_async_copy(blocks.at[half], packed.at[half], sems.at[3 + by]))
        sent[by].start()
    for copy in sent:
        copy.wait()


def coarse_kernel(
    packed, material, channel, coolant, index, levels, scaled, cells, base, tables,
    labels, small, ids, steps, all_cells, all_base, sems,
):
    copies = [
        pltpu.make_async_copy(channel, labels.at[0], sems.at[0]),
        pltpu.make_async_copy(material, labels.at[1], sems.at[1]),
        pltpu.make_async_copy(index, ids, sems.at[2]),
        pltpu.make_async_copy(coolant, small, sems.at[3]),
        pltpu.make_async_copy(levels, steps, sems.at[4]),
    ]
    for copy in copies:
        copy.start()
    tables[...] = jnp.zeros_like(tables)
    for copy in copies:
        copy.wait()
    tables[1:2, 0:SEGS] = small[...]
    tables[2:3, 0:SEGS] = ids[...].astype(jnp.float32)
    which = tables[2:3, :].astype(jnp.int32)
    picked = jnp.zeros((1, 128), jnp.float32)
    for level in range(LEVELS):
        picked = jnp.where(which == level, steps[level], picked)
    picked = jnp.where(lanes(1) < SEGS, picked, 0.0)
    heat = picked * tables[1:2, :]
    rate_table = pltpu.roll(picked, 1, 1)
    tables[0:1, :] = rate_table
    tables[1:2, :] = pltpu.roll(heat, 1, 1)
    tables[2:3, :] = pltpu.roll(picked, YB, 1)

    core = lax.axis_index("tm") & 1
    rest = jnp.where(core == 0, labels[0], labels[1]).astype(jnp.float32)
    rest = [window(rest, by) for by in range(2)]
    for b in range(16):
        for i in range(ZB // 8):
            at = slice(8 * i, 8 * i + 8)
            to = slice(ZB * b + 8 * i, ZB * b + 8 * i + 8)
            row = ZB * (b % 8) + 8 * i
            mine, theirs = packed[b, 1, at], rest[b // 8][row : row + 8]
            segs = jnp.where(core == 0, theirs, mine).astype(jnp.int32)
            lump = 1.0 + lump_rate * conductivity(jnp.where(core == 0, mine, theirs))
            scaled[to] = packed[b, 0, at] / (lump + lookup(rate_table, segs))
            all_cells[to] = segs
            all_base[to] = lump
    part = lax.axis_index("tm")
    for i in range(SOLVED // 8):
        rows = pl.ds(8 * PARTS * i + part, 8, stride=PARTS)
        cells[8 * i : 8 * i + 8] = all_cells[rows, :]
        base[8 * i : 8 * i + 8] = all_base[rows, :]


def strided(ref, pitch, at, half):
    return ref[pl.ds(half * pitch + at, 8, stride=2 * pitch), :]


def turned(i, count):
    return i + (lax.axis_index("tm") & 1) * (count - 1 - 2 * i)


def operator_rows(refs, spans, load, tables):
    cond, rate, kz, ky, kx, grow, heat, cavity = refs
    core = lax.axis_index("tm") & 1
    bz, by = lax.rem(lax.axis_index("space"), 8), lax.div(lax.axis_index("space"), 8)
    lane = lanes(8)
    sub = lax.broadcasted_iota(jnp.int32, (8, 128), 0)
    rate_table = tables[0:1, :]
    heat_table = tables[1:2, :]

    for fresh, _, _ in spans:
        for z in fresh:
            for half in range(2):
                to = slice(8 * half, 8 * half + 8)
                a, b = load(z, half)
                mat = jnp.where(core == 0, a, b)
                seg = jnp.where(core == 0, b, a).astype(jnp.int32)
                cond[z, to] = conductivity(mat)
                cavity[z, to] = jnp.where(mat == 2.0, time_step * melt_rate, 0.0)
                heat[z, to] = time_step * lookup(heat_table, seg)
                rate[z, to] = 1.0 + time_step * lookup(rate_table, seg)

    last = jnp.where(by == 0, 127, YB - 1)
    first = jnp.where(by == 0, 0, YB)
    y_inner = jnp.where(lane == last, 0.0, 0.5 * time_step)
    y_edge = jnp.where((lane == last) | (lane == first), time_step, 0.0)
    x_inner = jnp.where(sub == 7, 0.0, 0.5 * time_step)
    edges = (jnp.where(sub == 0, time_step, 0.0), jnp.where(sub == 7, time_step, 0.0))
    z0 = bz * ZB - HALO
    pairs = chebyshev()
    for _, faces, before in spans:
        flow = [None, None] if before is None else [kz[before, 0:8], kz[before, 8:16]]
        for z in faces:
            gz = z0 + turned(z, ZE)
            between_z = gz - core
            inner = jnp.where((between_z == -1) | (between_z == CZ - 1), 0.0, 0.5 * time_step)
            z_edge = jnp.where((gz == 0) | (gz == CZ - 1), time_step, 0.0)
            even, odd = cond[z, 0:8], cond[z, 8:16]
            between = (0.5 * time_step) * (even + odd)
            beyond = x_inner * (odd + pltpu.roll(even, 7, 0))
            kx[z, 0:8] = between
            kx[z, 8:16] = beyond
            across = (between + pltpu.roll(beyond, 1, 0), between + beyond)
            for half in range(2):
                at = slice(8 * half, 8 * half + 8)
                c = (even, odd)[half]
                high = inner * (c + cond[z + 1, at])
                kz[z, at] = high
                side = y_inner * (c + pltpu.roll(c, 127, 1))
                ky[z, at] = side
                if flow[half] is not None:
                    total = across[half] + side + pltpu.roll(side, 1, 1) + high + flow[half]
                    total = total + c * (edges[half] + y_edge + z_edge)
                    diag = rate[z, at] + total
                    grow[0, z, at] = 1.0 + (1.0 - diag) * (1.0 / cheb_center)
                    for sweep, (a, b) in enumerate(pairs):
                        grow[sweep + 1, z, at] = (1.0 + a) - b * diag
                flow[half] = high


def operator_core_kernel(received, other, tables, *refs):
    refs, scaled = refs[:8], refs[8]

    def load(z, half):
        z = turned(z - HALO, ZB)
        return strided(received, 2 * ZB, z + ZB, half), strided(other, HALO + ZB, HALO + z, half)

    spans = [(range(HALO, HALO + ZB), range(HALO, HALO + ZB - 1), None)]
    operator_rows(refs, spans, load, tables)
    core = lax.axis_index("tm") & 1
    for z in range(ZB):
        for half in range(2):
            a, b = load(HALO + z, half)
            seg = jnp.where(core == 0, b, a).astype(jnp.int32)
            at = slice(8 * half, 8 * half + 8)
            lump = 1.0 + lump_rate * refs[0][HALO + z, at]
            scaled[z, at] = strided(received, 2 * ZB, turned(z, ZB), half) / (lump + lookup(tables[0:1, :], seg))


def sweep_rows(buffers, operator, heated, j, spans):
    xa, xb, rhs = buffers
    kz, ky, kx, grow, heat, cavity = operator
    pairs = chebyshev()
    sweep = j % SWEEPS
    now, new = (xa, xb) if j % 2 == 0 else (xb, xa)
    halves = [slice(0, 8), slice(8, 16)]
    results = []
    for begin, end in spans:
        xs = {z: [now[z, at] for at in halves] for z in range(begin - 1, end + 1)}
        flows = {z: [kz[z, at] for at in halves] for z in range(begin - 1, end)}
        for z in range(begin, end):
            even, odd = xs[z]
            between, beyond = kx[z, 0:8], kx[z, 8:16]
            across = (
                between * odd + pltpu.roll(beyond * odd, 1, 0),
                between * even + beyond * pltpu.roll(even, 7, 0),
            )
            for half, at in enumerate(halves):
                v, side, keep = xs[z][half], ky[z, at], grow[sweep, z, at]
                total = flows[z][half] * xs[z + 1][half] + flows[z - 1][half] * xs[z - 1][half]
                total = across[half] + total
                total = total + (side * pltpu.roll(v, 127, 1) + pltpu.roll(side * v, 1, 1))
                if sweep == 0:
                    source = heat[z, at] + heated * cavity[z, at]
                    results.append((rhs, z, at, v + source))
                    value = keep * v + (total + source) * (1.0 / cheb_center)
                else:
                    a, b = pairs[sweep - 1]
                    value = (keep * v - a * new[z, at]) + b * (total + rhs[z, at])
                results.append((new, z, at, value))
    for ref, z, at, value in results:
        ref[z, at] = value


def melting(melt, j):
    return jnp.where(j // SWEEPS < melt[0], 1.0, 0.0)


def fine_core_kernel(melt, received, kz, ky, kx, grow, heat, cavity, xa, xb, rhs):
    for z in range(ZB):
        row = turned(z, ZB)
        xa[HALO + z, 0:8] = strided(received, 2 * ZB, row, 0)
        xa[HALO + z, 8:16] = strided(received, 2 * ZB, row, 1)
    for j in range(EARLY):
        spans = [(HALO + j + 1, HALO + ZB - j - 1)]
        sweep_rows((xa, xb, rhs), (kz, ky, kx, grow, heat, cavity), melting(melt, j), j, spans)


def rim_sweeps(melt, halo, tables, refs, spans, mine, other):
    operator, buffers = refs[:8], refs[8:]
    start = spans[0][0][0]

    def load(part, z, half):
        return strided(halo, HALO, 16 * HALO * part + turned(z - start, HALO), half)

    operator_rows(operator, spans, lambda z, half: (load(mine, z, half), load(other, z, half)), tables)
    for z in spans[0][0]:
        buffers[0][z, 0:8] = load(0, z, 0)
        buffers[0][z, 8:16] = load(0, z, 1)
    for j in range(EARLY):
        rows = (j + 1, HALO + j + 1) if start == 0 else (HALO + ZB - j - 1, ZE - 1 - j)
        sweep_rows(buffers, operator[2:], melting(melt, j), j, [rows])


def fine_upper_kernel(melt, rim, tables, *refs):
    rim_sweeps(melt, rim, tables, refs[11:], [(range(0, HALO), range(0, HALO + 1), None)], 2, 3)


def fine_lower_kernel(melt, back, scaled, tables, *refs):
    out, refs = refs[11], refs[12:]
    ends = HALO + ZB
    rim_sweeps(melt, back, tables, refs, [(range(ends, ZE), range(ends - 1, ZE - 1), ends - 2)], 2, 1)
    buffers, j = refs[8:], HALO - 1
    sweep_rows(buffers, refs[2:8], melting(melt, j), j, [(HALO, HALO + ZB)])
    lane = lanes(8)
    rates = tables[2:3, :]
    for z in range(ZB):
        row = turned(z, ZB)
        for half in range(2):
            at = slice(8 * half, 8 * half + 8)
            value = buffers[0][HALO + z, at] - scaled[z, at]
            first = 3 * (16 * (row & (PARTS - 1)) + half) + (row >> 4)
            out[pl.ds(first, 8, stride=6), :] = jnp.where(lane < YB, value, rates)


def cycle_kernel(offsets, cells, base, out):
    count = SOLVED // 8
    tiles = range(count)
    lane = lanes(8)
    ids = [cells[8 * i : 8 * i + 8] for i in tiles]
    lump = [base[8 * i : 8 * i + 8] for i in tiles]
    fixed = [v > 0 for v in ids]
    spots = [jnp.where(fixed[i], ids[i] + (YB - 1), 0) for i in tiles]
    gain = [jnp.ones((8, 128), jnp.float32)] * count
    shift = [jnp.zeros((8, 128), jnp.float32)] * count
    gains = []

    def given(g, i):
        return offsets[SOLVED * g + 8 * i : SOLVED * g + 8 * i + 8]

    for g in range(NT):
        table = offsets[SOLVED * g : SOLVED * g + 1, :]
        row = [
            1.0 / (lump[i] + jnp.where(fixed[i], lookup(table, spots[i]), 0.0)) for i in tiles
        ]
        gains.append(row)
        for i in tiles:
            gain[i] = row[i] * gain[i]
            shift[i] = row[i] * shift[i] + given(g, i)
    value = [shift[i] / (1.0 - gain[i]) for i in tiles]
    for g in range(NT):
        for i in tiles:
            side = pltpu.roll(given(g, 3 + i % 3), 96 if i < 3 else 64, 1)
            out[g, 8 * i : 8 * i + 8] = jnp.where(lane < YB, value[i], side)
        for i in range(3):
            side = pltpu.roll(given(g, 3 + i), 32, 1)
            out[g, SOLVED + 8 * i : SOLVED + 8 * i + 8] = jnp.where(lane < YB, given(g, i), side)
        for i in tiles:
            value[i] = gains[g][i] * value[i] + given(g, i)


def unpack_kernel(folded, scaled, starts, ends, new, fine):
    lane = lanes(8)
    for part in range(PARTS):
        for i in range(SOLVED // 8):
            rows = pl.ds(8 * PARTS * i + part, 8, stride=PARTS)
            new[rows, :] = folded[part, 8 * i : 8 * i + 8]
            if i < 3:
                fine[rows, :] = folded[part, SOLVED + 8 * i : SOLVED + 8 * i + 8]
            else:
                side = [folded[part, 24 * k + 8 * (i - 3) : 24 * k + 8 * (i - 3) + 8] for k in range(3)]
                side = [pltpu.roll(side[k], 32 + 32 * k, 1) for k in range(3)]
                fine[rows, :] = jnp.where(lane < 32, side[0], jnp.where(lane < 64, side[1], side[2]))
    for by in range(2):
        at, to = slice(CZ * by, CZ * by + CZ), slice(YB * by, YB * by + YB)
        starts[to, :] = new[at].T[0:YB]
        ends[to, :] = (fine[at] + scaled[at]).T[0:YB]


VMEM = pl.BlockSpec(memory_space=pltpu.VMEM)
SMEM = pl.BlockSpec(memory_space=pltpu.SMEM)
HBM = pl.BlockSpec(memory_space=pl.ANY)


def call(kernel, outs, in_specs, out_specs=None, scratch=(), limit=8, aliases={}, flops=0, nbytes=0):
    return pl.pallas_call(
        kernel,
        out_shape=outs,
        in_specs=in_specs,
        out_specs=out_specs or jax.tree.map(lambda _: VMEM, outs),
        scratch_shapes=list(scratch),
        input_output_aliases=aliases,
        compiler_params=pltpu.CompilerParams(vmem_limit_bytes=limit * 1024 * 1024),
        cost_estimate=pl.CostEstimate(flops=flops, bytes_accessed=nbytes, transcendentals=0),
    )


def f32(*shape):
    return jax.ShapeDtypeStruct(shape, jnp.float32)


def i32(*shape):
    return jax.ShapeDtypeStruct(shape, jnp.int32)


def per_device(start_guess, material, channel, coolant_temp, htc_index, htc_levels, melt_steps):
    labels = (material[0], channel[0])
    packed = call(
        pack_kernel,
        f32(16, 2, ZB, 128),
        [HBM] * 3,
        out_specs=HBM,
        limit=LIMIT,
        scratch=[
            pltpu.VMEM((CY, CZ), jnp.float32),
            pltpu.VMEM((2, CY, CZ), jnp.int32),
            pltpu.VMEM((16, 2, ZB, 128), jnp.float32),
            pltpu.SemaphoreType.DMA((5,)),
        ],
        nbytes=2000000,
    )(start_guess[0, 0], *labels)

    received = lax.all_to_all(packed, "space", 0, 0, tiled=True)

    swap = [(i, i ^ 1) for i in range(NT)]
    ahead = [
        (16 * tm + 8 * h + i + tm % 2, 16 * tm + 8 * h + i + 1 - tm % 2)
        for tm in range(NT)
        for h in range(2)
        for i in range(7)
    ]
    first_core = (lax.axis_index("tm") & 1) == 0
    field, label = received[:, 0], received[:, 1]
    top, bottom = slice(0, HALO), slice(HALO, ZB)
    away = jnp.where(first_core, field[:, top], field[:, bottom])
    other = lax.ppermute(jnp.concatenate([away, label], axis=1), "tm", swap)
    other_label = other[:, HALO:]
    sent = [
        jnp.where(first_core, field[:, bottom], field[:, top]),
        other[:, :HALO],
        jnp.where(first_core, label[:, bottom], label[:, top]),
        jnp.where(first_core, other_label[:, bottom], other_label[:, top]),
    ]
    rim = lax.ppermute(jnp.stack(sent), ("tm", "space"), ahead)

    flat = lambda v: v.reshape(-1, 128)
    plane = f32(ZE, 16, 128)
    planes = (plane,) * 5 + (f32(SWEEPS, ZE, 16, 128),) + (plane,) * 2
    received = flat(received)
    scaled, cells, base, tables = call(
        coarse_kernel,
        (f32(16 * ZB, 128), i32(SOLVED, 128), f32(SOLVED, 128), f32(8, 128)),
        [VMEM] + [HBM] * 5,
        scratch=[
            pltpu.VMEM((2, CY, CZ), jnp.int32),
            pltpu.VMEM((1, SEGS), jnp.float32),
            pltpu.VMEM((1, SEGS), jnp.int32),
            pltpu.SMEM((LEVELS,), jnp.float32),
            pltpu.VMEM((16 * ZB, 128), jnp.int32),
            pltpu.VMEM((16 * ZB, 128), jnp.float32),
            pltpu.SemaphoreType.DMA((5,)),
        ],
        nbytes=2000000,
    )(packed, *labels, coolant_temp, htc_index, htc_levels)
    *operator, own_scaled = call(operator_core_kernel, planes + (f32(ZB, 16, 128),), [VMEM] * 3)(
        received, flat(other), tables
    )
    fields = call(
        fine_core_kernel, (plane,) * 3, [SMEM] + [VMEM] * 7
    )(melt_steps, received, *operator[2:])
    rim, first, scaled = lax.optimization_barrier((rim, fields[0], scaled))
    fields = (first,) + tuple(fields[1:])
    back = flat(lax.ppermute(rim[1:4], "tm", swap))
    rim = flat(rim)
    state = call(
        fine_upper_kernel,
        planes + (plane,) * 3,
        [SMEM] + [VMEM] * 13,
        aliases={3 + i: i for i in range(11)},
        flops=20000000,
        nbytes=4000000,
    )(melt_steps, rim, tables, *operator, *fields)
    offsets = call(
        fine_lower_kernel,
        (f32(256 * 3, 128),) + planes + (plane,) * 3,
        [SMEM] + [VMEM] * 14,
        aliases={4 + i: 1 + i for i in range(11)},
        flops=20000000,
        nbytes=4000000,
    )(melt_steps, back, own_scaled, tables, *state)[0]

    offsets = lax.all_to_all(offsets.reshape(256, 1, 384), ("tm", "space"), 0, 0, tiled=True)
    both = call(cycle_kernel, f32(NT, 72, 128), [VMEM] * 3, nbytes=2000000)(
        flat(offsets), cells, base
    )
    both = lax.all_to_all(both, "tm", 0, 0, tiled=True)
    starts, ends = call(
        unpack_kernel,
        (f32(CY, CZ), f32(CY, CZ)),
        [VMEM] * 2,
        scratch=[pltpu.VMEM((16 * ZB, 128), jnp.float32)] * 2,
        nbytes=2000000,
    )(both, scaled)
    return starts[None, None], ends[None, None]


def solution(mesh):
    return jax.shard_map(
        per_device,
        mesh=mesh,
        in_specs=(
            P("tm", "space", None, None),
            P("space", None, None),
            P("space", None, None),
            P("tm", None),
            P("tm", None),
            P(),
            P("tm"),
        ),
        out_specs=(P("tm", "space", None, None), P("tm", "space", None, None)),
        check_vma=False,
    )
```

```python
import jax
import jax.numpy as jnp
from jax import lax
from jax.experimental import pallas as pl
from jax.experimental.pallas import tpu as pltpu
from jax.sharding import PartitionSpec as P

NT = 16
NX = 16
CY = 192
CZ = 384
STEPS = 4
SWEEPS = 6
SEGS = 32
LEVELS = 16

time_step = 0.25
melt_rate = 4.0
lam_high = 1.0 + time_step * (12.0 * 3.0 + 8.0)
cheb_center = 0.5 * (lam_high + 1.0)
cheb_half = 0.5 * (lam_high - 1.0)
cheb_ratio = cheb_center / cheb_half
lump_rate = 0.1 / NT

ZB = 48
HALO = STEPS * SWEEPS
ZE = ZB + 2 * HALO
YB = 96
PARTS = 16
SOLVED = ZB // PARTS * 16
EARLY = 23
LIMIT = 60


def chebyshev():
    rho = 1.0 / cheb_ratio
    pairs = []
    for _ in range(SWEEPS - 1):
        rho_next = 1.0 / (2.0 * cheb_ratio - rho)
        pairs.append((rho_next * rho, 2.0 * rho_next / cheb_half))
        rho = rho_next
    return pairs


def lanes(rows):
    return lax.broadcasted_iota(jnp.int32, (rows, 128), 1)


def lookup(row, index):
    return jnp.take_along_axis(jnp.broadcast_to(row, index.shape), index, axis=1, mode="promise_in_bounds")


def conductivity(material):
    return jnp.where(material == 0.0, 1.0, jnp.where(material == 1.0, 3.0, 0.6)).astype(jnp.float32)


def window(plane, by):
    part = plane[64 * by : 64 * by + 128, :].T
    return part if by == 0 else pltpu.roll(part, 96, 1)


def pack_kernel(start, material, channel, packed, fields, labels, blocks, sems):
    copies = [
        pltpu.make_async_copy(channel, labels.at[0], sems.at[0]),
        pltpu.make_async_copy(material, labels.at[1], sems.at[1]),
        pltpu.make_async_copy(start, fields, sems.at[2]),
    ]
    for copy in copies:
        copy.start()
    core = lax.axis_index("tm") & 1
    copies[0].wait()
    copies[1].wait()
    label = jnp.where(core == 0, labels[1], labels[0]).astype(jnp.float32)
    sent = []

    def send(by, field, block):
        for bz in range(8):
            blocks[8 * by + bz, field] = block[ZB * bz : ZB * bz + ZB]
        part = (pl.ds(8 * by, 8), field)
        copy = pltpu.make_async_copy(blocks.at[part], packed.at[part], sems.at[3 + 2 * field + by])
        copy.start()
        sent.append(copy)

    for by in range(2):
        send(by, 1, window(label, by))
    copies[2].wait()
    for by in range(2):
        send(by, 0, window(fields[...], by))
    for copy in sent:
        copy.wait()


def coarse_kernel(
    packed, material, channel, coolant, index, levels, scaled, cells, base, tables,
    labels, small, ids, steps, all_cells, all_base, sems,
):
    copies = [
        pltpu.make_async_copy(channel, labels.at[0], sems.at[0]),
        pltpu.make_async_copy(material, labels.at[1], sems.at[1]),
        pltpu.make_async_copy(index, ids, sems.at[2]),
        pltpu.make_async_copy(coolant, small, sems.at[3]),
        pltpu.make_async_copy(levels, steps, sems.at[4]),
    ]
    for copy in copies:
        copy.start()
    tables[...] = jnp.zeros_like(tables)
    for copy in copies:
        copy.wait()
    tables[1:2, 0:SEGS] = small[...]
    tables[2:3, 0:SEGS] = ids[...].astype(jnp.float32)
    which = tables[2:3, :].astype(jnp.int32)
    picked = jnp.zeros((1, 128), jnp.float32)
    for level in range(LEVELS):
        picked = jnp.where(which == level, steps[level], picked)
    picked = jnp.where(lanes(1) < SEGS, picked, 0.0)
    heat = picked * tables[1:2, :]
    rate_table = pltpu.roll(picked, 1, 1)
    tables[0:1, :] = rate_table
    tables[1:2, :] = pltpu.roll(heat, 1, 1)
    tables[2:3, :] = pltpu.roll(picked, YB, 1)

    core = lax.axis_index("tm") & 1
    rest = jnp.where(core == 0, labels[0], labels[1]).astype(jnp.float32)
    rest = [window(rest, by) for by in range(2)]
    for b in range(16):
        for i in range(ZB // 8):
            at = slice(8 * i, 8 * i + 8)
            to = slice(ZB * b + 8 * i, ZB * b + 8 * i + 8)
            row = ZB * (b % 8) + 8 * i
            mine, theirs = packed[b, 1, at], rest[b // 8][row : row + 8]
            segs = jnp.where(core == 0, theirs, mine).astype(jnp.int32)
            lump = 1.0 + lump_rate * conductivity(jnp.where(core == 0, mine, theirs))
            scaled[to] = packed[b, 0, at] / (lump + lookup(rate_table, segs))
            all_cells[to] = segs
            all_base[to] = lump
    part = lax.axis_index("tm")
    for i in range(SOLVED // 8):
        rows = pl.ds(8 * PARTS * i + part, 8, stride=PARTS)
        cells[8 * i : 8 * i + 8] = all_cells[rows, :]
        base[8 * i : 8 * i + 8] = all_base[rows, :]


def strided(ref, pitch, at, half):
    return ref[pl.ds(half * pitch + at, 8, stride=2 * pitch), :]


def turned(i, count):
    return i + (lax.axis_index("tm") & 1) * (count - 1 - 2 * i)


def operator_rows(refs, spans, load, tables):
    cond, rate, kz, ky, kx, grow, heat, cavity = refs
    core = lax.axis_index("tm") & 1
    bz, by = lax.rem(lax.axis_index("space"), 8), lax.div(lax.axis_index("space"), 8)
    lane = lanes(8)
    sub = lax.broadcasted_iota(jnp.int32, (8, 128), 0)
    rate_table = tables[0:1, :]
    heat_table = tables[1:2, :]

    for fresh, _, _ in spans:
        for z in fresh:
            for half in range(2):
                to = slice(8 * half, 8 * half + 8)
                a, b = load(z, half)
                mat = jnp.where(core == 0, a, b)
                seg = jnp.where(core == 0, b, a).astype(jnp.int32)
                cond[z, to] = conductivity(mat)
                cavity[z, to] = jnp.where(mat == 2.0, time_step * melt_rate, 0.0)
                heat[z, to] = time_step * lookup(heat_table, seg)
                rate[z, to] = 1.0 + time_step * lookup(rate_table, seg)

    last = jnp.where(by == 0, 127, YB - 1)
    first = jnp.where(by == 0, 0, YB)
    y_inner = jnp.where(lane == last, 0.0, 0.5 * time_step)
    y_edge = jnp.where((lane == last) | (lane == first), time_step, 0.0)
    x_inner = jnp.where(sub == 7, 0.0, 0.5 * time_step)
    edges = (jnp.where(sub == 0, time_step, 0.0), jnp.where(sub == 7, time_step, 0.0))
    z0 = bz * ZB - HALO
    pairs = chebyshev()
    for _, faces, before in spans:
        flow = [None, None] if before is None else [kz[before, 0:8], kz[before, 8:16]]
        for z in faces:
            gz = z0 + turned(z, ZE)
            between_z = gz - core
            inner = jnp.where((between_z == -1) | (between_z == CZ - 1), 0.0, 0.5 * time_step)
            z_edge = jnp.where((gz == 0) | (gz == CZ - 1), time_step, 0.0)
            even, odd = cond[z, 0:8], cond[z, 8:16]
            between = (0.5 * time_step) * (even + odd)
            beyond = x_inner * (odd + pltpu.roll(even, 7, 0))
            kx[z, 0:8] = between
            kx[z, 8:16] = beyond
            across = (between + pltpu.roll(beyond, 1, 0), between + beyond)
            for half in range(2):
                at = slice(8 * half, 8 * half + 8)
                c = (even, odd)[half]
                high = inner * (c + cond[z + 1, at])
                kz[z, at] = high
                side = y_inner * (c + pltpu.roll(c, 127, 1))
                ky[z, at] = side
                if flow[half] is not None:
                    total = across[half] + side + pltpu.roll(side, 1, 1) + high + flow[half]
                    total = total + c * (edges[half] + y_edge + z_edge)
                    diag = rate[z, at] + total
                    grow[0, z, at] = 1.0 + (1.0 - diag) * (1.0 / cheb_center)
                    for sweep, (a, b) in enumerate(pairs):
                        grow[sweep + 1, z, at] = (1.0 + a) - b * diag
                flow[half] = high


def operator_core_kernel(received, other, tables, *refs):
    refs, scaled = refs[:8], refs[8]

    def load(z, half):
        z = turned(z - HALO, ZB)
        return strided(received, 2 * ZB, z + ZB, half), strided(other, HALO + ZB, HALO + z, half)

    spans = [(range(HALO, HALO + ZB), range(HALO, HALO + ZB - 1), None)]
    operator_rows(refs, spans, load, tables)
    core = lax.axis_index("tm") & 1
    for z in range(ZB):
        for half in range(2):
            a, b = load(HALO + z, half)
            seg = jnp.where(core == 0, b, a).astype(jnp.int32)
            at = slice(8 * half, 8 * half + 8)
            lump = 1.0 + lump_rate * refs[0][HALO + z, at]
            scaled[z, at] = strided(received, 2 * ZB, turned(z, ZB), half) / (lump + lookup(tables[0:1, :], seg))


def sweep_rows(buffers, operator, heated, j, spans):
    xa, xb, rhs = buffers
    kz, ky, kx, grow, heat, cavity = operator
    pairs = chebyshev()
    sweep = j % SWEEPS
    now, new = (xa, xb) if j % 2 == 0 else (xb, xa)
    halves = [slice(0, 8), slice(8, 16)]
    results = []
    for begin, end in spans:
        xs = {z: [now[z, at] for at in halves] for z in range(begin - 1, end + 1)}
        flows = {z: [kz[z, at] for at in halves] for z in range(begin - 1, end)}
        for z in range(begin, end):
            even, odd = xs[z]
            between, beyond = kx[z, 0:8], kx[z, 8:16]
            across = (
                between * odd + pltpu.roll(beyond * odd, 1, 0),
                between * even + beyond * pltpu.roll(even, 7, 0),
            )
            for half, at in enumerate(halves):
                v, side, keep = xs[z][half], ky[z, at], grow[sweep, z, at]
                total = flows[z][half] * xs[z + 1][half] + flows[z - 1][half] * xs[z - 1][half]
                total = across[half] + total
                total = total + (side * pltpu.roll(v, 127, 1) + pltpu.roll(side * v, 1, 1))
                if sweep == 0:
                    source = heat[z, at] + heated * cavity[z, at]
                    results.append((rhs, z, at, v + source))
                    value = keep * v + (total + source) * (1.0 / cheb_center)
                else:
                    a, b = pairs[sweep - 1]
                    value = (keep * v - a * new[z, at]) + b * (total + rhs[z, at])
                results.append((new, z, at, value))
    for ref, z, at, value in results:
        ref[z, at] = value


def melting(melt, j):
    return jnp.where(j // SWEEPS < melt[0], 1.0, 0.0)


def fine_core_kernel(melt, received, kz, ky, kx, grow, heat, cavity, xa, xb, rhs):
    for z in range(ZB):
        row = turned(z, ZB)
        xa[HALO + z, 0:8] = strided(received, 2 * ZB, row, 0)
        xa[HALO + z, 8:16] = strided(received, 2 * ZB, row, 1)
    for j in range(EARLY):
        spans = [(HALO + j + 1, HALO + ZB - j - 1)]
        sweep_rows((xa, xb, rhs), (kz, ky, kx, grow, heat, cavity), melting(melt, j), j, spans)


def rim_sweeps(melt, halo, tables, refs, spans, mine, other):
    operator, buffers = refs[:8], refs[8:]
    start = spans[0][0][0]

    def load(part, z, half):
        return strided(halo, HALO, 16 * HALO * part + turned(z - start, HALO), half)

    operator_rows(operator, spans, lambda z, half: (load(mine, z, half), load(other, z, half)), tables)
    for z in spans[0][0]:
        buffers[0][z, 0:8] = load(0, z, 0)
        buffers[0][z, 8:16] = load(0, z, 1)
    for j in range(EARLY):
        rows = (j + 1, HALO + j + 1) if start == 0 else (HALO + ZB - j - 1, ZE - 1 - j)
        sweep_rows(buffers, operator[2:], melting(melt, j), j, [rows])


def fine_upper_kernel(melt, rim, tables, *refs):
    rim_sweeps(melt, rim, tables, refs[11:], [(range(0, HALO), range(0, HALO + 1), None)], 2, 3)


def fine_lower_kernel(melt, back, scaled, tables, *refs):
    out, refs = refs[11], refs[12:]
    ends = HALO + ZB
    rim_sweeps(melt, back, tables, refs, [(range(ends, ZE), range(ends - 1, ZE - 1), ends - 2)], 2, 1)
    buffers, j = refs[8:], HALO - 1
    sweep_rows(buffers, refs[2:8], melting(melt, j), j, [(HALO, HALO + ZB)])
    lane = lanes(8)
    rates = tables[2:3, :]
    for z in range(ZB):
        row = turned(z, ZB)
        for half in range(2):
            at = slice(8 * half, 8 * half + 8)
            value = buffers[0][HALO + z, at] - scaled[z, at]
            first = 3 * (16 * (row & (PARTS - 1)) + half) + (row >> 4)
            out[pl.ds(first, 8, stride=6), :] = jnp.where(lane < YB, value, rates)


def cycle_kernel(offsets, cells, base, out):
    count = SOLVED // 8
    tiles = range(count)
    lane = lanes(8)
    ids = [cells[8 * i : 8 * i + 8] for i in tiles]
    lump = [base[8 * i : 8 * i + 8] for i in tiles]
    fixed = [v > 0 for v in ids]
    spots = [jnp.where(fixed[i], ids[i] + (YB - 1), 0) for i in tiles]
    gain = [jnp.ones((8, 128), jnp.float32)] * count
    shift = [jnp.zeros((8, 128), jnp.float32)] * count
    gains = []

    def given(g, i):
        return offsets[SOLVED * g + 8 * i : SOLVED * g + 8 * i + 8]

    for g in range(NT):
        table = offsets[SOLVED * g : SOLVED * g + 1, :]
        row = [
            1.0 / (lump[i] + jnp.where(fixed[i], lookup(table, spots[i]), 0.0)) for i in tiles
        ]
        gains.append(row)
        for i in tiles:
            gain[i] = row[i] * gain[i]
            shift[i] = row[i] * shift[i] + given(g, i)
    value = [shift[i] / (1.0 - gain[i]) for i in tiles]
    for g in range(NT):
        for i in tiles:
            side = pltpu.roll(given(g, 3 + i % 3), 96 if i < 3 else 64, 1)
            out[g, 8 * i : 8 * i + 8] = jnp.where(lane < YB, value[i], side)
        for i in range(3):
            side = pltpu.roll(given(g, 3 + i), 32, 1)
            out[g, SOLVED + 8 * i : SOLVED + 8 * i + 8] = jnp.where(lane < YB, given(g, i), side)
        for i in tiles:
            value[i] = gains[g][i] * value[i] + given(g, i)


def unpack_kernel(folded, scaled, starts, ends, new, fine):
    lane = lanes(8)
    for part in range(PARTS):
        for i in range(SOLVED // 8):
            rows = pl.ds(8 * PARTS * i + part, 8, stride=PARTS)
            new[rows, :] = folded[part, 8 * i : 8 * i + 8]
            if i < 3:
                fine[rows, :] = folded[part, SOLVED + 8 * i : SOLVED + 8 * i + 8]
            else:
                side = [folded[part, 24 * k + 8 * (i - 3) : 24 * k + 8 * (i - 3) + 8] for k in range(3)]
                side = [pltpu.roll(side[k], 32 + 32 * k, 1) for k in range(3)]
                fine[rows, :] = jnp.where(lane < 32, side[0], jnp.where(lane < 64, side[1], side[2]))
    for by in range(2):
        at, to = slice(CZ * by, CZ * by + CZ), slice(YB * by, YB * by + YB)
        starts[to, :] = new[at].T[0:YB]
        ends[to, :] = (fine[at] + scaled[at]).T[0:YB]


VMEM = pl.BlockSpec(memory_space=pltpu.VMEM)
SMEM = pl.BlockSpec(memory_space=pltpu.SMEM)
HBM = pl.BlockSpec(memory_space=pl.ANY)


def call(kernel, outs, in_specs, out_specs=None, scratch=(), limit=8, aliases={}, flops=0, nbytes=0):
    return pl.pallas_call(
        kernel,
        out_shape=outs,
        in_specs=in_specs,
        out_specs=out_specs or jax.tree.map(lambda _: VMEM, outs),
        scratch_shapes=list(scratch),
        input_output_aliases=aliases,
        compiler_params=pltpu.CompilerParams(vmem_limit_bytes=limit * 1024 * 1024),
        cost_estimate=pl.CostEstimate(flops=flops, bytes_accessed=nbytes, transcendentals=0),
    )


def f32(*shape):
    return jax.ShapeDtypeStruct(shape, jnp.float32)


def i32(*shape):
    return jax.ShapeDtypeStruct(shape, jnp.int32)


def per_device(start_guess, material, channel, coolant_temp, htc_index, htc_levels, melt_steps):
    labels = (material[0], channel[0])
    packed = call(
        pack_kernel,
        f32(16, 2, ZB, 128),
        [HBM] * 3,
        out_specs=HBM,
        limit=LIMIT,
        scratch=[
            pltpu.VMEM((CY, CZ), jnp.float32),
            pltpu.VMEM((2, CY, CZ), jnp.int32),
            pltpu.VMEM((16, 2, ZB, 128), jnp.float32),
            pltpu.SemaphoreType.DMA((7,)),
        ],
        nbytes=2000000,
    )(start_guess[0, 0], *labels)

    received = lax.all_to_all(packed, "space", 0, 0, tiled=True)

    swap = [(i, i ^ 1) for i in range(NT)]
    ahead = [
        (16 * tm + 8 * h + i + tm % 2, 16 * tm + 8 * h + i + 1 - tm % 2)
        for tm in range(NT)
        for h in range(2)
        for i in range(7)
    ]
    first_core = (lax.axis_index("tm") & 1) == 0
    field, label = received[:, 0], received[:, 1]
    top, bottom = slice(0, HALO), slice(HALO, ZB)
    away = jnp.where(first_core, field[:, top], field[:, bottom])
    other = lax.ppermute(jnp.concatenate([away, label], axis=1), "tm", swap)
    other_label = other[:, HALO:]
    sent = [
        jnp.where(first_core, field[:, bottom], field[:, top]),
        other[:, :HALO],
        jnp.where(first_core, label[:, bottom], label[:, top]),
        jnp.where(first_core, other_label[:, bottom], other_label[:, top]),
    ]
    rim = lax.ppermute(jnp.stack(sent), ("tm", "space"), ahead)

    flat = lambda v: v.reshape(-1, 128)
    plane = f32(ZE, 16, 128)
    planes = (plane,) * 5 + (f32(SWEEPS, ZE, 16, 128),) + (plane,) * 2
    received = flat(received)
    scaled, cells, base, tables = call(
        coarse_kernel,
        (f32(16 * ZB, 128), i32(SOLVED, 128), f32(SOLVED, 128), f32(8, 128)),
        [VMEM] + [HBM] * 5,
        scratch=[
            pltpu.VMEM((2, CY, CZ), jnp.int32),
            pltpu.VMEM((1, SEGS), jnp.float32),
            pltpu.VMEM((1, SEGS), jnp.int32),
            pltpu.SMEM((LEVELS,), jnp.float32),
            pltpu.VMEM((16 * ZB, 128), jnp.int32),
            pltpu.VMEM((16 * ZB, 128), jnp.float32),
            pltpu.SemaphoreType.DMA((5,)),
        ],
        nbytes=2000000,
    )(packed, *labels, coolant_temp, htc_index, htc_levels)
    *operator, own_scaled = call(operator_core_kernel, planes + (f32(ZB, 16, 128),), [VMEM] * 3)(
        received, flat(other), tables
    )
    fields = call(
        fine_core_kernel, (plane,) * 3, [SMEM] + [VMEM] * 7
    )(melt_steps, received, *operator[2:])
    rim, first, scaled = lax.optimization_barrier((rim, fields[0], scaled))
    fields = (first,) + tuple(fields[1:])
    back = flat(lax.ppermute(rim[1:4], "tm", swap))
    rim = flat(rim)
    state = call(
        fine_upper_kernel,
        planes + (plane,) * 3,
        [SMEM] + [VMEM] * 13,
        aliases={3 + i: i for i in range(11)},
        flops=20000000,
        nbytes=4000000,
    )(melt_steps, rim, tables, *operator, *fields)
    offsets = call(
        fine_lower_kernel,
        (f32(256 * 3, 128),) + planes + (plane,) * 3,
        [SMEM] + [VMEM] * 14,
        aliases={4 + i: 1 + i for i in range(11)},
        flops=20000000,
        nbytes=4000000,
    )(melt_steps, back, own_scaled, tables, *state)[0]

    offsets = lax.all_to_all(offsets.reshape(256, 1, 384), ("tm", "space"), 0, 0, tiled=True)
    both = call(cycle_kernel, f32(NT, 72, 128), [VMEM] * 3, nbytes=2000000)(
        flat(offsets), cells, base
    )
    both = lax.all_to_all(both, "tm", 0, 0, tiled=True)
    starts, ends = call(
        unpack_kernel,
        (f32(CY, CZ), f32(CY, CZ)),
        [VMEM] * 2,
        scratch=[pltpu.VMEM((16 * ZB, 128), jnp.float32)] * 2,
        nbytes=2000000,
    )(both, scaled)
    return starts[None, None], ends[None, None]


def solution(mesh):
    return jax.shard_map(
        per_device,
        mesh=mesh,
        in_specs=(
            P("tm", "space", None, None),
            P("space", None, None),
            P("space", None, None),
            P("tm", None),
            P("tm", None),
            P(),
            P("tm"),
        ),
        out_specs=(P("tm", "space", None, None), P("tm", "space", None, None)),
        check_vma=False,
    )
```
